512 devices in a mesh: ha: 16 (over y, x), wa: 16 (over z), col: 2 (over core).
Axes of the slice: x: 4, y: 4, z: 16, core: 2. Of those that a mesh axis runs over, the one named last changes fastest.
Arguments:
- inputs: bfloat16 [2, 12, 16, 24576], P('col', None, 'ha', 'wa'), may hold values from -6 to 6
- carried: bfloat16 [2, 2, 16, 24576], P('col', None, 'ha', 'wa'), may hold values from -6 to 6
- gain: float32 [192], replicated, may hold values from 0.1 to 1.9
- weight: bfloat16 [27, 36864], replicated, may hold values from -0.078125 to 0.078125
- cotangent: bfloat16 [2, 12, 32, 49152], P('col', None, 'ha', 'wa'), may hold values from -4 to 4
Outputs:
- grad_inputs: bfloat16 [2, 12, 16, 24576], P('col', None, 'ha', 'wa')
- grad_weight: float32 [2, 27, 18432], P('col', None, ('ha', 'wa'))
- grad_gain: float32 [192], replicated
The draws below stay inside these ranges and needn't reach their ends.
All inputs are finite; a program needn't handle non-finite values.
Results may differ from the reference program's by a relative error of at most 0.0017.
Values may be sent and summed in bfloat16 or wider, within the bound.
A program may use at most 64 MiB of HBM per device.

```python
import jax
import jax.numpy as jnp
from jax import lax

CH = 192
FRAMES = 12
CLIPS = 2
HL = 16
WL = 128


def steps_of(stream_key, dims, shards, least, top_value):
    def one(axis_at, shards_of):
        steps = jax.random.uniform(jax.random.fold_in(jax.random.fold_in(stream_key, 6), axis_at), (shards_of,), jnp.float32, least / len(shards), top_value / len(shards))
        return jnp.repeat(jnp.exp(steps), dims[axis_at] // shards_of).reshape((-1,) + (1,) * (len(dims) - axis_at - 1))

    loudness = one(*shards[0])
    for cut in shards[1:]:
        loudness = loudness * one(*cut)
    return loudness


def normal_values(rng, extent, deviation, most, cuts=(), kind=jnp.bfloat16):
    level = steps_of(rng, extent, cuts, -0.22, 0.18) if cuts else 1.0
    array = jax.random.normal(rng, extent, jnp.float32) * deviation * level
    return jnp.minimum(jnp.maximum(array, -most), most).astype(kind)


def setup_inputs(seed: int = 0) -> dict:
    streams_of = jax.random.split(jax.random.key(seed), 6)
    return {
        "inputs": normal_values(streams_of[0], (CLIPS, FRAMES, HL, WL * CH), 1.0, 6.0, ((0, 2), (2, 16), (3, 16))),
        "carried": normal_values(streams_of[1], (CLIPS, 2, HL, WL * CH), 1.0, 6.0, ((0, 2), (2, 16), (3, 16))),
        "gain": jnp.clip(1.0 + 0.18 * jax.random.normal(streams_of[2], (CH,), jnp.float32), 0.1, 1.9),
        "weight": normal_values(streams_of[3], (27, CH * CH), (27 * CH) ** -0.5, 0.078125),
        "cotangent": normal_values(streams_of[4], (CLIPS, FRAMES, 2 * HL, 2 * WL * CH), 0.25, 4.0, ((0, 2), (2, 16), (3, 16))),
    }


def prepare(inputs, gain):
    values = inputs.astype(jnp.float32)
    scale = lax.rsqrt(lax.optimization_barrier(jnp.mean(values * values, axis=-1, keepdims=True)) + 1e-06)
    normed = values * scale
    act = normed * gain
    activated = jax.nn.silu(act).astype(jnp.bfloat16)
    return (scale, normed, act, activated)

def upsample(field):
    return jnp.repeat(jnp.repeat(field, 2, axis=2), 2, axis=3)

def reference(inputs, carried, gain, weight, cotangent):
    inputs = inputs.reshape(CLIPS, FRAMES, HL, WL, CH)
    carried = carried.reshape(CLIPS, 2, HL, WL, CH)
    cotangent = cotangent.reshape(CLIPS, FRAMES, 2 * HL, 2 * WL, CH)
    kernel = weight.reshape(3, 3, 3, CH, CH)
    scale, normed, act, activated = prepare(inputs, gain)
    frames = jnp.concatenate([carried, activated], axis=1)
    upper = jnp.pad(upsample(frames), ((0, 0), (0, 0), (1, 1), (1, 1), (0, 0)))
    lower = jnp.pad(cotangent, ((0, 0), (0, 2), (1, 1), (1, 1), (0, 0)))
    height = 2 * HL
    breadth = 2 * WL
    cot_flat = cotangent.reshape(-1, CH)
    tap_terms = []
    back_field = jnp.zeros(cotangent.shape, jnp.float32)
    for t_shift in range(3):
        for h_shift in range(3):
            for w_shift in range(3):
                piece = upper[:, t_shift:t_shift + FRAMES, h_shift:h_shift + height, w_shift:w_shift + breadth, :].reshape(-1, CH)
                tap_terms.append(lax.dot_general(piece, cot_flat, (((0,), (0,)), ((), ())), preferred_element_type=jnp.float32))
                source = lower[:, 2 - t_shift:2 - t_shift + FRAMES, 2 - h_shift:2 - h_shift + height, 2 - w_shift:2 - w_shift + breadth, :].reshape(-1, CH)
                product = lax.dot_general(source, kernel[t_shift, h_shift, w_shift], (((1,), (1,)), ((), ())), preferred_element_type=jnp.float32)
                back_field = back_field + product.reshape(cotangent.shape)
    full_term = jnp.stack(tap_terms).reshape(27, 2, CH // 2 * CH)
    grad_weight = jnp.transpose(full_term, (1, 0, 2))
    coarse = back_field.reshape(CLIPS, FRAMES, HL, 2, WL, 2, CH).sum(axis=(3, 5))
    sigmoid_act = jax.nn.sigmoid(act)
    grad_act = coarse * sigmoid_act * (1.0 + act * (1.0 - sigmoid_act))
    grad_gain = lax.optimization_barrier(jnp.sum(grad_act * normed, axis=(0, 1, 2, 3)))
    grad_normed = grad_act * gain
    grad_inputs = scale * (grad_normed - normed * lax.optimization_barrier(jnp.mean(grad_normed * normed, axis=-1, keepdims=True)))
    grad_inputs = grad_inputs.astype(jnp.bfloat16).reshape(CLIPS, FRAMES, HL, WL * CH)
    return (grad_inputs, grad_weight, grad_gain)
```

```python
import functools

import jax
import jax.numpy as jnp
from jax import lax
from jax.experimental import pallas as pl
from jax.experimental.pallas import tpu as pltpu
from jax.sharding import PartitionSpec as P

CH = 192
T = 12
S = 8
TP = 16
ROWS = S * TP
HALF = 896
MESH = pl.DeviceIdType.MESH
F32 = jnp.float32
BF16 = jnp.bfloat16
NT = (((1,), (1,)), ((), ()))


def remote(src, dst, send, recv, device):
    return pltpu.make_async_remote_copy(
        src_ref=src, dst_ref=dst, send_sem=send, recv_sem=recv, device_id=device, device_id_type=MESH
    )


def kernel(
    x_ref, car_ref, gain_ref, w_ref, cot_ref,
    gi_ref, gw_ref, gg_ref,
    wv, ws, wte, wto, rws, cs, colh, uf, ut, dk, de, do, p, r1, t2, q2, r2, vs, zb, r3, gh, gz, gc,
    w_sem, halo_s, halo_r, core_s, core_r, s1s, s1r, s2s, s2r, s3s, s3r, ghs, ghr, gzs, gzr, gcs, gcr,
):
    ha = lax.axis_index("ha")
    wa = lax.axis_index("wa")
    col = lax.axis_index("col")
    qy, qx = ha // 4, ha % 4
    up, down = (ha + 15) % 16, (ha + 1) % 16
    left, right = (wa + 15) % 16, (wa + 1) % 16
    other = 1 - col

    barrier = pltpu.get_barrier_semaphore()

    def greet(d, _):
        pl.semaphore_signal(barrier, inc=1, device_id=((ha + d) % 16, wa, col), device_id_type=MESH)
        pl.semaphore_signal(barrier, inc=1, device_id=(ha, (wa + d) % 16, col), device_id_type=MESH)
        return 0

    lax.fori_loop(1, 16, greet, 0)
    pl.semaphore_signal(barrier, inc=1, device_id=(ha, wa, other), device_id_type=MESH)
    for h in (up, down):
        for w in (left, right):
            pl.semaphore_signal(barrier, inc=1, device_id=(h, w, col), device_id_type=MESH)

    w_copy = pltpu.make_async_copy(w_ref, wv, w_sem)
    w_copy.start()

    pad4 = jnp.zeros((TP - T, 2 * S * CH), F32)
    for row in range(2):
        value = cot_ref[:, row, :].astype(F32)
        value = jnp.concatenate([value, pad4], axis=0).astype(BF16)
        rws[1 + row] = value
        cs[0, row, :, 0:CH] = value[:, 0:CH]
        cs[1, row, :, 0:CH] = value[:, 15 * CH : 16 * CH]

    pl.semaphore_wait(barrier, 35)

    halos = []

    def halo(src, dst, device):
        n = len(halos)
        copy = remote(src, dst, halo_s.at[n], halo_r.at[n], device)
        copy.start()
        halos.append(copy)

    halo(rws.at[1], rws.at[3], (up, wa, col))
    halo(rws.at[2], rws.at[0], (down, wa, col))
    halo(cs.at[0], colh.at[1, pl.ds(1, 2)], (ha, left, col))
    halo(cs.at[1], colh.at[0, pl.ds(1, 2)], (ha, right, col))
    halo(cs.at[0, 0], colh.at[1, 3], (up, left, col))
    halo(cs.at[1, 0], colh.at[0, 3], (up, right, col))
    halo(cs.at[0, 1], colh.at[1, 0], (down, left, col))
    halo(cs.at[1, 1], colh.at[0, 0], (down, right, col))

    gain = gain_ref[...]
    pad = jnp.zeros((TP - T, CH), F32)
    x = jnp.concatenate(
        [piece for s in range(S) for piece in (x_ref[:, s * CH : (s + 1) * CH].astype(F32), pad)], axis=0
    )
    scale = lax.rsqrt(jnp.mean(x * x, axis=-1, keepdims=True) + 1e-06)
    normed = x * scale
    act = normed * gain
    sig = 1.0 / (1.0 + jnp.exp(-act))
    activated = (act * sig).astype(BF16).astype(F32).reshape(S, TP, CH)
    for s in range(S):
        uf[s, 0:2, :] = car_ref[:, s * CH : (s + 1) * CH].astype(F32)
        uf[s, 2 : 2 + TP, :] = activated[s]

    m = lax.broadcasted_iota(jnp.int32, (CH, CH), 0)
    lane = lax.broadcasted_iota(jnp.int32, (CH, CH), 1)
    mm = jnp.where(m >= 96, m - 96, m)
    first = (mm >= 24).astype(jnp.int32) + (mm >= 48).astype(jnp.int32) + (mm >= 72).astype(jnp.int32)
    rest = mm - 24 * first
    second = (rest >= 6).astype(jnp.int32) + (rest >= 12).astype(jnp.int32) + (rest >= 18).astype(jnp.int32)
    swapped = 24 * second + 6 * first + (rest - 6 * second)
    channel = jnp.where(m >= 96, swapped, mm)
    for k, half in ((0, col), (1, other)):
        sel = (lane == channel + 96 * half).astype(F32).astype(BF16)
        for a in range(3):
            u = uf[:, a : a + TP, :].reshape(ROWS, CH).astype(BF16)
            ut[2 * k, a] = lax.dot_general(sel, u, NT, preferred_element_type=F32).astype(BF16)
    u_copy = remote(ut.at[2], ut.at[1], core_s.at[0], core_r.at[0], (ha, wa, other))
    u_copy.start()

    for copy in halos:
        copy.wait_recv()
    top = (ha > 0).astype(F32)
    bottom = (ha < 15).astype(F32)
    at_left = (wa > 0).astype(F32)
    at_right = (wa < 15).astype(F32)
    zero64 = jnp.zeros((TP, 64), BF16)
    dk[0 : 2 * ROWS, 9 * CH :] = jnp.zeros((2 * ROWS, 2 * HALF - 9 * CH), BF16)
    for b in range(3):
        lo_row, hi_row = ((2, 3), (1, 2), (0, 1))[b]

        def rows_of(load):
            one, two = load(lo_row).astype(F32), load(hi_row).astype(F32)
            if b == 0:
                two = two * bottom
            if b == 2:
                one = one * top
            return one + two

        cols = {}
        for j in range(2 * S):
            cols[j] = rows_of(lambda r: rws[r, :, j * CH : (j + 1) * CH])
        cols[-1] = rows_of(lambda r: colh[0, r, :, 0:CH]) * at_left
        cols[2 * S] = rows_of(lambda r: colh[1, r, :, 0:CH]) * at_right
        for e in range(3):
            be = 3 * b + e
            for s in range(S):
                j = 2 * s + 1 - e
                d = cols[j] + cols[j + 1]
                high = d.astype(BF16)
                low = (d - high.astype(F32)).astype(BF16)
                for k, part in ((0, high), (1, low)):
                    at = k * ROWS + s * TP
                    dk[at : at + TP, be * CH : (be + 1) * CH] = part
                    de[at : at + TP, be * 256 : (be + 1) * 256] = jnp.concatenate([part, zero64], axis=1)
                    do[at : at + TP, be * 256 : (be + 1) * 256] = jnp.concatenate([zero64, part], axis=1)
    d_copies = []
    for hf in range(2):
        lanes = pl.ds(hf * HALF, HALF)
        copy = remote(
            dk.at[pl.ds(0, 2 * ROWS), lanes], dk.at[pl.ds(2 * ROWS, 2 * ROWS), lanes],
            core_s.at[1 + hf], core_r.at[1 + hf], (ha, wa, other),
        )
        copy.start()
        d_copies.append(copy)

    w_copy.wait()

    def widen(n, _):
        lanes = pl.ds(pl.multiple_of(n * 128, 128), 128)
        for t8 in range(4):
            count = 8 if t8 < 3 else 3
            at = pl.multiple_of((t8 * 288 + n) * 8, 8)
            ws[pl.ds(at, count), :] = wv[t8 * 8 : t8 * 8 + count, lanes].astype(F32)
        return 0

    lax.fori_loop(0, 288, widen, 0, unroll=8)
    for a in range(3):
        wte[a * 128 + 96 : (a + 1) * 128, :] = jnp.zeros((32, 9 * 256), BF16)
        wto[a * 128 + 96 : (a + 1) * 128, :] = jnp.zeros((32, 9 * 256), BF16)
        for be in range(9):
            t8, tr = (9 * a + be) // 8, (9 * a + be) % 8
            tiles = [ws[pl.ds((t8 * 288 + j) * 8 + tr, 96, stride=24), :].astype(BF16) for j in range(3)]
            rows = slice(a * 128, a * 128 + 96)
            wte[rows, be * 256 : be * 256 + 128] = tiles[0]
            wte[rows, be * 256 + 128 : be * 256 + 256] = tiles[1]
            wto[rows, be * 256 : be * 256 + 128] = tiles[1]
            wto[rows, be * 256 + 128 : be * 256 + 256] = tiles[2]

    def ring(hf, d):
        if hf == 0:
            return ((qy + d) % 4) * 4 + qx
        return qy * 4 + (qx + d) % 4

    mine = (qy, qx)
    u_copy.wait_recv()
    ones = {}
    for hf in range(2):
        d_copies[hf].wait_recv()
        for a in range(3):
            rows = slice(hf * 96, hf * 96 + 96)
            own, his = ut[0, a, rows, :], ut[1, a, rows, :]
            lhs = jnp.concatenate([own, own, his, his], axis=1)
            part = jnp.dot(lhs, dk[:, hf * HALF : (hf + 1) * HALF], preferred_element_type=F32)
            p[a, hf] = part.reshape(4, 24, HALF)
            for d in range(1, 4):
                copy = remote(
                    p.at[a, hf, (mine[hf] + d) % 4], r1.at[a, hf, d - 1], s1s.at[a, hf, d - 1], s1r.at[a, hf, d - 1],
                    (ring(hf, d), wa, col),
                )
                copy.start()
                ones[a, hf, d] = copy

    coarse = None
    pair = lax.broadcasted_iota(jnp.int32, (128, CH), 0)
    chan = lax.broadcasted_iota(jnp.int32, (128, CH), 1)
    for parity, (lhs_ref, rhs_ref) in enumerate(((de, wte), (do, wto))):
        g = lax.dot_general(lhs_ref[...], rhs_ref[...], NT, preferred_element_type=F32)
        g = g[0:ROWS] + g[ROWS : 2 * ROWS]
        g = (
            g[:, 256:384]
            + pltpu.roll(g[:, 128:256], ROWS - 1, axis=0)
            + pltpu.roll(g[:, 0:128], ROWS - 2, axis=0)
        )
        spread = (chan == 2 * pair + parity).astype(F32)
        g = jnp.dot(g, spread, precision=lax.Precision.HIGHEST, preferred_element_type=F32)
        coarse = g if coarse is None else coarse + g
    grad_act = coarse * (sig * (1.0 + act * (1.0 - sig)))
    gain_term = jnp.sum(grad_act * normed, axis=0, keepdims=True)
    gh[ha] = jnp.concatenate([gain_term, jnp.zeros((1, 64), F32)], axis=1)
    gh_copies = []

    def gh_send(d, _):
        remote(gh.at[ha], gh.at[ha], ghs.at[d - 1], ghr.at[d - 1], ((ha + d) % 16, wa, col)).start()
        return 0

    lax.fori_loop(1, 16, gh_send, 0)
    grad_normed = grad_act * gain
    grad_in = scale * (grad_normed - normed * jnp.mean(grad_normed * normed, axis=-1, keepdims=True))
    for s in range(S):
        gi_ref[:, s * CH : (s + 1) * CH] = grad_in[s * TP : s * TP + T].astype(BF16)

    twos = {}
    for a in range(3):
        for hf in range(2):
            for d in range(1, 4):
                ones[a, hf, d].wait_recv()
            total = p[a, hf, mine[hf]] + r1[a, hf, 0] + r1[a, hf, 1] + r1[a, hf, 2]
            t2[0:24, :] = total
            t2[24:32, :] = jnp.zeros((8, HALF), F32)
            for k in range(4):
                q2[a, hf, k] = t2[6 * k : 6 * k + 8, :]
            for d in range(1, 4):
                copy = remote(
                    q2.at[a, hf, (mine[1 - hf] + d) % 4], r2.at[a, hf, d - 1], s2s.at[a, hf, d - 1],
                    s2r.at[a, hf, d - 1], (ring(1 - hf, d), wa, col),
                )
                copy.start()
                twos[a, hf, d] = copy

    def gh_wait(d, _):
        src = (ha + 16 - d) % 16
        remote(gh.at[ha], gh.at[src], ghs.at[d - 1], ghr.at[d - 1], (src, wa, col)).wait_recv()
        return 0

    lax.fori_loop(1, 16, gh_wait, 0)
    gz[wa] = jnp.sum(gh[...], axis=0)

    def gz_send(d, _):
        remote(gz.at[wa], gz.at[wa], gzs.at[d - 1], gzr.at[d - 1], (ha, (wa + d) % 16, col)).start()
        return 0

    lax.fori_loop(1, 16, gz_send, 0)

    for a in range(3):
        for hf in range(2):
            for d in range(1, 4):
                twos[a, hf, d].wait_recv()
            total = q2[a, hf, mine[1 - hf]] + r2[a, hf, 0] + r2[a, hf, 1] + r2[a, hf, 2]
            for k in range(7):
                at = (7 * hf + k) * 8
                vs[a, at : at + 8, :] = total[:, k * 128 : (k + 1) * 128]
        vs[a, 112:192, :] = jnp.zeros((80, 128), F32)
        y = []
        for i in range(6):
            tiles = jnp.concatenate([vs[a, pl.ds(j * 8 + i, 8, stride=24), :] for j in range(3)], axis=1)
            y.append((tiles[:, 0:CH], tiles[:, CH : 2 * CH]))
        for w in range(16):
            i0, o0 = (72 * w) // CH, (72 * w) % CH
            n0 = min(72, CH - o0)
            pieces = []
            for parity in range(2):
                pieces.append(y[i0][parity][:, o0 : o0 + n0])
                if n0 < 72:
                    pieces.append(y[i0 + 1][parity][:, 0 : 72 - n0])
            tile = jnp.concatenate(pieces, axis=1)
            zb[a, w] = tile[:, 0:128]
            spare = jnp.concatenate([tile[k : k + 1, 128:144] for k in range(4)], axis=1)
            zb[a, w, 5:6, 0:64] = spare

        def z_send(d, _):
            remote(
                zb.at[a, (wa + d) % 16], r3.at[a, d - 1], s3s.at[a, d - 1], s3r.at[a, d - 1],
                (ha, (wa + d) % 16, col),
            ).start()
            return 0

        lax.fori_loop(1, 16, z_send, 0)

    def gz_wait(d, _):
        src = (wa + 16 - d) % 16
        remote(gz.at[wa], gz.at[src], gzs.at[d - 1], gzr.at[d - 1], (ha, src, col)).wait_recv()
        return 0

    lax.fori_loop(1, 16, gz_wait, 0)
    gc[0] = jnp.sum(gz[...], axis=0)
    gc_copy = remote(gc.at[0], gc.at[1], gcs, gcr, (ha, wa, other))
    gc_copy.start()

    for a in range(3):

        def z_wait(d, _):
            remote(
                zb.at[a, (wa + d) % 16], r3.at[a, d - 1], s3s.at[a, d - 1], s3r.at[a, d - 1],
                (ha, (wa + d) % 16, col),
            ).wait()
            return 0

        lax.fori_loop(1, 16, z_wait, 0)
        total = zb[a, wa] + jnp.sum(r3[a], axis=0)
        for be in range(9):
            k = be // 2
            if be % 2 == 0:
                row = total[k : k + 1, 0:72]
            else:
                row = jnp.concatenate([total[k : k + 1, 72:128], total[5:6, 16 * k : 16 * k + 16]], axis=1)
            gw_ref[9 * a + be : 9 * a + be + 1, :] = row

    gc_copy.wait()
    gg_ref[...] = (gc[0] + gc[1])[:, 0:CH]

    for copy in halos + d_copies + [u_copy] + list(ones.values()) + list(twos.values()):
        copy.wait_send()

    def g_done(d, _):
        remote(gh.at[ha], gh.at[ha], ghs.at[d - 1], ghr.at[d - 1], ((ha + d) % 16, wa, col)).wait_send()
        remote(gz.at[wa], gz.at[wa], gzs.at[d - 1], gzr.at[d - 1], (ha, (wa + d) % 16, col)).wait_send()
        return 0

    lax.fori_loop(1, 16, g_done, 0)


def on_device(inputs, carried, gain, weight, cotangent):
    vmem = pl.BlockSpec(memory_space=pltpu.VMEM)
    dma = pltpu.SemaphoreType.DMA
    gi, gw, gg = pl.pallas_call(
        kernel,
        out_shape=(
            jax.ShapeDtypeStruct((T, S * CH), BF16),
            jax.ShapeDtypeStruct((27, 72), F32),
            jax.ShapeDtypeStruct((1, CH), F32),
        ),
        in_specs=[vmem, vmem, vmem, pl.BlockSpec(memory_space=pl.ANY), vmem],
        out_specs=(vmem, vmem, vmem),
        scratch_shapes=[
            pltpu.VMEM((27, CH * CH), BF16),
            pltpu.VMEM((4 * 288 * 8, 128), F32),
            pltpu.VMEM((384, 9 * 256), BF16),
            pltpu.VMEM((384, 9 * 256), BF16),
            pltpu.VMEM((4, TP, 2 * S * CH), BF16),
            pltpu.VMEM((2, 2, TP, 256), BF16),
            pltpu.VMEM((2, 4, TP, 256), BF16),
            pltpu.VMEM((S, 24, CH), F32),
            pltpu.VMEM((3, 3, CH, ROWS), BF16),
            pltpu.VMEM((4 * ROWS, 2 * HALF), BF16),
            pltpu.VMEM((2 * ROWS, 9 * 256), BF16),
            pltpu.VMEM((2 * ROWS, 9 * 256), BF16),
            pltpu.VMEM((3, 2, 4, 24, HALF), F32),
            pltpu.VMEM((3, 2, 3, 24, HALF), F32),
            pltpu.VMEM((32, HALF), F32),
            pltpu.VMEM((3, 2, 4, 8, HALF), F32),
            pltpu.VMEM((3, 2, 3, 8, HALF), F32),
            pltpu.VMEM((3, 192, 128), F32),
            pltpu.VMEM((3, 16, 8, 128), F32),
            pltpu.VMEM((3, 15, 8, 128), F32),
            pltpu.VMEM((16, 1, 256), F32),
            pltpu.VMEM((16, 1, 256), F32),
            pltpu.VMEM((2, 1, 256), F32),
            dma(()), dma((8,)), dma((8,)), dma((3,)), dma((3,)),
            dma((3, 2, 3)), dma((3, 2, 3)), dma((3, 2, 3)), dma((3, 2, 3)),
            dma((3, 15)), dma((3, 15)), dma((15,)), dma((15,)), dma((15,)), dma((15,)), dma(()), dma(()),
        ],
        compiler_params=pltpu.CompilerParams(
            collective_id=0, has_side_effects=True, vmem_limit_bytes=50 * 1024 * 1024
        ),
    )(
        inputs.reshape(T, S * CH),
        carried.reshape(2, S * CH),
        gain.reshape(1, CH),
        weight,
        cotangent.reshape(T, 2, 2 * S * CH),
    )
    return gi.reshape(inputs.shape), gw.reshape(1, 27, 72), gg.reshape(CH)


def solution(mesh):
    placed = (
        P("col", None, "ha", "wa"),
        P("col", None, "ha", "wa"),
        P(),
        P(),
        P("col", None, "ha", "wa"),
    )
    return jax.shard_map(
        on_device,
        mesh=mesh,
        in_specs=placed,
        out_specs=(P("col", None, "ha", "wa"), P("col", None, ("ha", "wa")), P()),
        check_vma=False,
    )
```

```python
import functools

import jax
import jax.numpy as jnp
from jax import lax
from jax.experimental import pallas as pl
from jax.experimental.pallas import tpu as pltpu
from jax.sharding import PartitionSpec as P

CH = 192
T = 12
S = 8
TP = 16
ROWS = S * TP
HALF = 896
MESH = pl.DeviceIdType.MESH
F32 = jnp.float32
BF16 = jnp.bfloat16
NT = (((1,), (1,)), ((), ()))


def remote(src, dst, send, recv, device):
    return pltpu.make_async_remote_copy(
        src_ref=src, dst_ref=dst, send_sem=send, recv_sem=recv, device_id=device, device_id_type=MESH
    )


def kernel(
    x_hbm, car_hbm, gain_hbm, w_hbm, cot_hbm,
    gi_ref, gw_ref, gg_ref,
    x_ref, car_ref, gain_ref, cv, cf, fr, rb, hb, colh, wv, ws, wt, uf, ut, dk, p, r1, t2, q2, r2, vs, zb, r3,
    gh, gz, gc,
    in_sem, halo_s, halo_r, core_s, core_r, s1s, s1r, s2s, s2r, s3s, s3r, ghs, ghr, gzs, gzr, gcs, gcr,
):
    ha = lax.axis_index("ha")
    wa = lax.axis_index("wa")
    col = lax.axis_index("col")
    qy, qx = ha // 4, ha % 4
    up, down = (ha + 15) % 16, (ha + 1) % 16
    left, right = (wa + 15) % 16, (wa + 1) % 16
    other = 1 - col

    barrier = pltpu.get_barrier_semaphore()
    loads = [
        pltpu.make_async_copy(src, dst, in_sem.at[n])
        for n, (src, dst) in enumerate(
            ((cot_hbm, cv), (x_hbm, x_ref), (car_hbm, car_ref), (gain_hbm, gain_ref), (w_hbm, wv))
        )
    ]
    for load in loads:
        load.start()
    pl.semaphore_signal(barrier, inc=1, device_id=(ha, wa, other), device_id_type=MESH)
    for h in (up, down):
        for w in (left, right):
            pl.semaphore_signal(barrier, inc=1, device_id=(h, w, col), device_id_type=MESH)

    def greet(d, _):
        pl.semaphore_signal(barrier, inc=1, device_id=((ha + d) % 16, wa, col), device_id_type=MESH)
        pl.semaphore_signal(barrier, inc=1, device_id=(ha, (wa + d) % 16, col), device_id_type=MESH)
        return 0

    lax.fori_loop(1, 16, greet, 0)

    loads[0].wait()
    cf[...] = cv[...].astype(F32)
    pad4 = jnp.zeros((TP - T, 128), F32)
    for row in range(2):
        for lt in range(24):
            value = jnp.concatenate([cf[pl.ds(2 * lt + row, T, stride=48), :], pad4], axis=0)
            fr[row, lt] = value
            rb[row, lt] = value.astype(BF16)

    pl.semaphore_wait(barrier, 35)

    halos = []

    def halo(src, dst, device):
        n = len(halos)
        copy = remote(src, dst, halo_s.at[n], halo_r.at[n], device)
        copy.start()
        halos.append(copy)

    first_two, last_two = pl.ds(0, 2), pl.ds(22, 2)
    halo(rb.at[0], hb.at[1], (up, wa, col))
    halo(rb.at[1], hb.at[0], (down, wa, col))
    halo(rb.at[:, first_two], colh.at[1, pl.ds(1, 2)], (ha, left, col))
    halo(rb.at[:, last_two], colh.at[0, pl.ds(1, 2)], (ha, right, col))
    halo(rb.at[0, first_two], colh.at[1, 3], (up, left, col))
    halo(rb.at[0, last_two], colh.at[0, 3], (up, right, col))
    halo(rb.at[1, first_two], colh.at[1, 0], (down, left, col))
    halo(rb.at[1, last_two], colh.at[0, 0], (down, right, col))

    for load in loads[1:4]:
        load.wait()
    gain = gain_ref[...]
    pad = jnp.zeros((TP - T, CH), F32)
    x = jnp.concatenate(
        [piece for s in range(S) for piece in (x_ref[:, s * CH : (s + 1) * CH].astype(F32), pad)], axis=0
    )
    scale = lax.rsqrt(jnp.mean(x * x, axis=-1, keepdims=True) + 1e-06)
    normed = x * scale
    act = normed * gain
    sig = 1.0 / (1.0 + jnp.exp(-act))
    activated = (act * sig).astype(BF16).astype(F32).reshape(S, TP, CH)
    for s in range(S):
        uf[s, 0:2, :] = car_ref[:, s * CH : (s + 1) * CH].astype(F32)
        uf[s, 2 : 2 + TP, :] = activated[s]

    m = lax.broadcasted_iota(jnp.int32, (96, CH), 0)
    lane = lax.broadcasted_iota(jnp.int32, (96, CH), 1)
    first = (m >= 24).astype(jnp.int32) + (m >= 48).astype(jnp.int32) + (m >= 72).astype(jnp.int32)
    rest = m - 24 * first
    second = (rest >= 6).astype(jnp.int32) + (rest >= 12).astype(jnp.int32) + (rest >= 18).astype(jnp.int32)
    swapped = 24 * second + 6 * first + (rest - 6 * second)
    u = jnp.concatenate([uf[:, a : a + TP, :].reshape(ROWS, CH).astype(BF16) for a in range(3)], axis=0)
    for k, half in ((2, other), (0, col)):
        for hf, channel in enumerate((m, swapped)):
            sel = (lane == channel + 96 * half).astype(F32).astype(BF16)
            moved = lax.dot_general(sel, u, NT, preferred_element_type=F32).astype(BF16)
            for a in range(3):
                ut[k, hf, a] = moved[:, a * ROWS : (a + 1) * ROWS]
        if k == 2:
            u_copy = remote(ut.at[2], ut.at[1], core_s.at[0], core_r.at[0], (ha, wa, other))
            u_copy.start()

    for copy in halos:
        copy.wait_recv()
    top = (ha > 0).astype(F32)
    bottom = (ha < 15).astype(F32)
    at_left = (wa > 0).astype(F32)
    at_right = (wa < 15).astype(F32)
    low_lanes = lax.broadcasted_iota(jnp.int32, (TP, 128), 1) < 64

    def turn(tile):
        return pltpu.roll(tile, 64, axis=1)

    def row_sum(b, load):
        one, two = load(b)
        if b == 0:
            two = two * bottom
        if b == 2:
            one = one * top
        return one + two

    def own_rows(lt):
        def load(b):
            if b == 0:
                return fr[1, lt], hb[1, lt].astype(F32)
            if b == 1:
                return fr[0, lt], fr[1, lt]
            return hb[0, lt].astype(F32), fr[0, lt]

        return load

    def side_rows(side, k):
        def load(b):
            return colh[side, 2 - b, k].astype(F32), colh[side, 3 - b, k].astype(F32)

        return load

    columns = {}

    def column(b, j):
        if (b, j) not in columns:
            if j == -1:
                pair = [row_sum(b, side_rows(0, k)) * at_left for k in range(2)]
            elif j == 2 * S:
                pair = [row_sum(b, side_rows(1, k)) * at_right for k in range(2)]
            else:
                pair = [row_sum(b, own_rows(3 * (j // 2) + j % 2 + k)) for k in range(2)]
            turned = [turn(pair[0]), turn(pair[1])]
            if j % 2 == 0:
                moved = [turned[0], jnp.where(low_lanes, turned[0], turned[1])]
            else:
                moved = [jnp.where(low_lanes, turned[0], turned[1]), turned[1]]
            columns[b, j] = (pair, moved)
        return columns[b, j]

    def cells(be, s, k):
        b, e = be // 3, be % 3
        j = 2 * s + 1 - e
        total = None
        for c in (j, j + 1):
            natural, moved = column(b, c)
            tile = natural[k] if c % 2 == be % 2 else moved[k]
            total = tile if total is None else total + tile
        return total

    d_copies = []
    for hf in range(2):
        for s in range(S):
            for n in range(7 * hf, 7 * hf + 7):
                be, k = 2 * (n // 3), n % 3
                if k == 0:
                    tile = cells(be, s, 0)
                elif k == 1:
                    tile = jnp.where(low_lanes, cells(be, s, 1), cells(be + 1, s, 0) if be < 8 else 0.0)
                else:
                    tile = cells(be + 1, s, 1)
                high = tile.astype(BF16)
                low = (tile - high.astype(F32)).astype(BF16)
                dk[s * TP : (s + 1) * TP, n * 128 : (n + 1) * 128] = high
                dk[ROWS + s * TP : ROWS + (s + 1) * TP, n * 128 : (n + 1) * 128] = low
        lanes = pl.ds(hf * HALF, HALF)
        copy = remote(
            dk.at[pl.ds(0, 2 * ROWS), lanes], dk.at[pl.ds(2 * ROWS, 2 * ROWS), lanes],
            core_s.at[1 + hf], core_r.at[1 + hf], (ha, wa, other),
        )
        copy.start()
        d_copies.append(copy)

    loads[4].wait()

    def widen(n, _):
        lanes = pl.ds(pl.multiple_of(n * 128, 128), 128)
        for t8 in range(4):
            count = 8 if t8 < 3 else 3
            at = pl.multiple_of((t8 * 288 + n) * 8, 8)
            ws[pl.ds(at, count), :] = wv[t8 * 8 : t8 * 8 + count, lanes].astype(F32)
        return 0

    lax.fori_loop(0, 288, widen, 0, unroll=8)
    low_wide = lax.broadcasted_iota(jnp.int32, (96, 128), 1) < 64
    for a in range(3):
        for parity in range(2):
            at = a * 256 + parity * 128
            wt[at + 96 : at + 128, :] = jnp.zeros((32, 2 * HALF), BF16)
        even = slice(a * 256, a * 256 + 96)
        odd = slice(a * 256 + 128, a * 256 + 224)
        for k in range(5):

            def tap(be, j):
                t8, tr = (9 * a + be) // 8, (9 * a + be) % 8
                return ws[pl.ds((t8 * 288 + j) * 8 + tr, 96, stride=24), :]

            a0, a1, a2 = (tap(2 * k, j) for j in range(3))
            t1, t2w = turn(a1), turn(a2)
            at = k * 384
            wt[even, at : at + 128] = a0.astype(BF16)
            wt[odd, at : at + 128] = jnp.where(low_wide, t1, t2w).astype(BF16)
            if k < 4:
                b0, b1, b2 = (tap(2 * k + 1, j) for j in range(3))
                s0, s1 = turn(b0), turn(b1)
                wt[even, at + 128 : at + 256] = jnp.where(low_wide, a1, s0).astype(BF16)
                wt[even, at + 256 : at + 384] = jnp.where(low_wide, s0, s1).astype(BF16)
                wt[odd, at + 128 : at + 256] = jnp.where(low_wide, t2w, b1).astype(BF16)
                wt[odd, at + 256 : at + 384] = b2.astype(BF16)
            else:
                wt[even, at + 128 : at + 256] = jnp.where(low_wide, a1, 0.0).astype(BF16)
                wt[odd, at + 128 : at + 256] = jnp.where(low_wide, t2w, 0.0).astype(BF16)

    def ring(hf, d):
        if hf == 0:
            return ((qy + d) % 4) * 4 + qx
        return qy * 4 + (qx + d) % 4

    mine = (qy, qx)
    u_copy.wait_recv()
    ones = {}
    for hf in range(2):
        d_copies[hf].wait_recv()
        own, his = (ut[k, hf].reshape(288, ROWS) for k in range(2))
        lhs = jnp.concatenate([own, own, his, his], axis=1)
        part = jnp.dot(lhs, dk[:, hf * HALF : (hf + 1) * HALF], preferred_element_type=F32)
        p[hf] = part.reshape(3, 4, 24, HALF)
        for a in range(3):
            for d in range(1, 4):
                copy = remote(
                    p.at[hf, a, (mine[hf] + d) % 4], r1.at[a, hf, d - 1], s1s.at[a, hf, d - 1], s1r.at[a, hf, d - 1],
                    (ring(hf, d), wa, col),
                )
                copy.start()
                ones[a, hf, d] = copy

    g = lax.dot_general(dk[0 : 2 * ROWS, :], wt[...], NT, preferred_element_type=F32)
    g = g[0:ROWS] + g[ROWS : 2 * ROWS]
    g = g[:, 512:768] + pltpu.roll(g[:, 256:512], ROWS - 1, axis=0) + pltpu.roll(g[:, 0:256], ROWS - 2, axis=0)
    k = lax.broadcasted_iota(jnp.int32, (256, CH), 0)
    chan = lax.broadcasted_iota(jnp.int32, (256, CH), 1)
    spread = (chan == jnp.where(k < 128, 2 * k, 2 * (k - 128) + 1)).astype(F32).astype(BF16)
    high = g.astype(BF16)
    low = (g - high.astype(F32)).astype(BF16)
    coarse = jnp.dot(jnp.concatenate([high, low], axis=0), spread, preferred_element_type=F32)
    coarse = coarse[0:ROWS] + coarse[ROWS : 2 * ROWS]
    grad_act = coarse * (sig * (1.0 + act * (1.0 - sig)))
    gain_term = jnp.sum(grad_act * normed, axis=0, keepdims=True)
    gh[ha] = jnp.concatenate([gain_term, jnp.zeros((1, 64), F32)], axis=1)

    def gh_send(d, _):
        remote(gh.at[ha], gh.at[ha], ghs.at[d - 1], ghr.at[d - 1], ((ha + d) % 16, wa, col)).start()
        return 0

    lax.fori_loop(1, 16, gh_send, 0)
    grad_normed = grad_act * gain
    grad_in = scale * (grad_normed - normed * jnp.mean(grad_normed * normed, axis=-1, keepdims=True))
    for s in range(S):
        gi_ref[:, s * CH : (s + 1) * CH] = grad_in[s * TP : s * TP + T].astype(BF16)

    twos = {}
    for a in range(3):
        for hf in range(2):
            for d in range(1, 4):
                ones[a, hf, d].wait_recv()
            total = p[hf, a, mine[hf]] + r1[a, hf, 0] + r1[a, hf, 1] + r1[a, hf, 2]
            t2[0:24, :] = total
            t2[24:32, :] = jnp.zeros((8, HALF), F32)
            for k in range(4):
                q2[a, hf, k] = t2[6 * k : 6 * k + 8, :]
            for d in range(1, 4):
                copy = remote(
                    q2.at[a, hf, (mine[1 - hf] + d) % 4], r2.at[a, hf, d - 1], s2s.at[a, hf, d - 1],
                    s2r.at[a, hf, d - 1], (ring(1 - hf, d), wa, col),
                )
                copy.start()
                twos[a, hf, d] = copy

    def gh_wait(d, _):
        src = (ha + 16 - d) % 16
        remote(gh.at[ha], gh.at[src], ghs.at[d - 1], ghr.at[d - 1], (src, wa, col)).wait_recv()
        return 0

    lax.fori_loop(1, 16, gh_wait, 0)
    gz[wa] = jnp.sum(gh[...], axis=0)

    def gz_send(d, _):
        remote(gz.at[wa], gz.at[wa], gzs.at[d - 1], gzr.at[d - 1], (ha, (wa + d) % 16, col)).start()
        return 0

    lax.fori_loop(1, 16, gz_send, 0)

    for a in range(3):
        for hf in range(2):
            for d in range(1, 4):
                twos[a, hf, d].wait_recv()
            total = q2[a, hf, mine[1 - hf]] + r2[a, hf, 0] + r2[a, hf, 1] + r2[a, hf, 2]
            for k in range(7):
                at = (7 * hf + k) * 8
                vs[a, at : at + 8, :] = total[:, k * 128 : (k + 1) * 128]
        vs[a, 112:192, :] = jnp.zeros((80, 128), F32)
        y = []
        for i in range(6):
            tiles = jnp.concatenate([vs[a, pl.ds(j * 8 + i, 8, stride=24), :] for j in range(3)], axis=1)
            y.append((tiles[:, 0:CH], tiles[:, CH : 2 * CH]))
        for w in range(16):
            i0, o0 = (72 * w) // CH, (72 * w) % CH
            n0 = min(72, CH - o0)
            pieces = []
            for parity in range(2):
                pieces.append(y[i0][parity][:, o0 : o0 + n0])
                if n0 < 72:
                    pieces.append(y[i0 + 1][parity][:, 0 : 72 - n0])
            tile = jnp.concatenate(pieces, axis=1)
            zb[a, w] = tile[:, 0:128]
            spare = jnp.concatenate([tile[k : k + 1, 128:144] for k in range(4)], axis=1)
            zb[a, w, 5:6, 0:64] = spare

        def z_send(d, _):
            remote(
                zb.at[a, (wa + d) % 16], r3.at[a, d - 1], s3s.at[a, d - 1], s3r.at[a, d - 1],
                (ha, (wa + d) % 16, col),
            ).start()
            return 0

        lax.fori_loop(1, 16, z_send, 0)

    def gz_wait(d, _):
        src = (wa + 16 - d) % 16
        remote(gz.at[wa], gz.at[src], gzs.at[d - 1], gzr.at[d - 1], (ha, src, col)).wait_recv()
        return 0

    lax.fori_loop(1, 16, gz_wait, 0)
    gc[0] = jnp.sum(gz[...], axis=0)
    gc_copy = remote(gc.at[0], gc.at[1], gcs, gcr, (ha, wa, other))
    gc_copy.start()

    for a in range(3):

        def z_wait(d, _):
            remote(
                zb.at[a, (wa + d) % 16], r3.at[a, d - 1], s3s.at[a, d - 1], s3r.at[a, d - 1],
                (ha, (wa + d) % 16, col),
            ).wait()
            return 0

        lax.fori_loop(1, 16, z_wait, 0)
        total = zb[a, wa] + jnp.sum(r3[a], axis=0)
        for be in range(9):
            k = be // 2
            if be % 2 == 0:
                row = total[k : k + 1, 0:72]
            else:
                row = jnp.concatenate([total[k : k + 1, 72:128], total[5:6, 16 * k : 16 * k + 16]], axis=1)
            gw_ref[9 * a + be : 9 * a + be + 1, :] = row

    gc_copy.wait()
    gg_ref[...] = (gc[0] + gc[1])[:, 0:CH]

    for copy in halos + d_copies + [u_copy] + list(ones.values()) + list(twos.values()):
        copy.wait_send()

    def g_done(d, _):
        remote(gh.at[ha], gh.at[ha], ghs.at[d - 1], ghr.at[d - 1], ((ha + d) % 16, wa, col)).wait_send()
        remote(gz.at[wa], gz.at[wa], gzs.at[d - 1], gzr.at[d - 1], (ha, (wa + d) % 16, col)).wait_send()
        return 0

    lax.fori_loop(1, 16, g_done, 0)


def on_device(inputs, carried, gain, weight, cotangent):
    vmem = pl.BlockSpec(memory_space=pltpu.VMEM)
    hbm = pl.BlockSpec(memory_space=pl.ANY)
    dma = pltpu.SemaphoreType.DMA
    gi, gw, gg = pl.pallas_call(
        kernel,
        out_shape=(
            jax.ShapeDtypeStruct((T, S * CH), BF16),
            jax.ShapeDtypeStruct((27, 72), F32),
            jax.ShapeDtypeStruct((1, CH), F32),
        ),
        in_specs=[hbm] * 5,
        out_specs=(vmem, vmem, vmem),
        scratch_shapes=[
            pltpu.VMEM((T, S * CH), BF16),
            pltpu.VMEM((2, S * CH), BF16),
            pltpu.VMEM((1, CH), F32),
            pltpu.VMEM((576, 128), BF16),
            pltpu.VMEM((576, 128), F32),
            pltpu.VMEM((2, 24, TP, 128), F32),
            pltpu.VMEM((2, 24, TP, 128), BF16),
            pltpu.VMEM((2, 24, TP, 128), BF16),
            pltpu.VMEM((2, 4, 2, TP, 128), BF16),
            pltpu.VMEM((27, CH * CH), BF16),
            pltpu.VMEM((4 * 288 * 8, 128), F32),
            pltpu.VMEM((768, 2 * HALF), BF16),
            pltpu.VMEM((S, 24, CH), F32),
            pltpu.VMEM((3, 2, 3, 96, ROWS), BF16),
            pltpu.VMEM((4 * ROWS, 2 * HALF), BF16),
            pltpu.VMEM((2, 3, 4, 24, HALF), F32),
            pltpu.VMEM((3, 2, 3, 24, HALF), F32),
            pltpu.VMEM((32, HALF), F32),
            pltpu.VMEM((3, 2, 4, 8, HALF), F32),
            pltpu.VMEM((3, 2, 3, 8, HALF), F32),
            pltpu.VMEM((3, 192, 128), F32),
            pltpu.VMEM((3, 16, 8, 128), F32),
            pltpu.VMEM((3, 15, 8, 128), F32),
            pltpu.VMEM((16, 1, 256), F32),
            pltpu.VMEM((16, 1, 256), F32),
            pltpu.VMEM((2, 1, 256), F32),
            dma((5,)), dma((8,)), dma((8,)), dma((3,)), dma((3,)),
            dma((3, 2, 3)), dma((3, 2, 3)), dma((3, 2, 3)), dma((3, 2, 3)),
            dma((3, 15)), dma((3, 15)), dma((15,)), dma((15,)), dma((15,)), dma((15,)), dma(()), dma(()),
        ],
        compiler_params=pltpu.CompilerParams(
            collective_id=0, has_side_effects=True, vmem_limit_bytes=60 * 1024 * 1024
        ),
    )(
        inputs.reshape(T, S * CH),
        carried.reshape(2, S * CH),
        gain.reshape(1, CH),
        weight,
        cotangent.reshape(T, 2, 24, 128).transpose(0, 2, 1, 3).reshape(576, 128),
    )
    return gi.reshape(inputs.shape), gw.reshape(1, 27, 72), gg.reshape(CH)


def solution(mesh):
    placed = (
        P("col", None, "ha", "wa"),
        P("col", None, "ha", "wa"),
        P(),
        P(),
        P("col", None, "ha", "wa"),
    )
    return jax.shard_map(
        on_device,
        mesh=mesh,
        in_specs=placed,
        out_specs=(P("col", None, "ha", "wa"), P("col", None, ("ha", "wa")), P()),
        check_vma=False,
    )
```

```python
import functools

import jax
import jax.numpy as jnp
from jax import lax
from jax.experimental import pallas as pl
from jax.experimental.pallas import tpu as pltpu
from jax.sharding import PartitionSpec as P

CH = 192
T = 12
S = 8
TP = 16
ROWS = S * TP
HALF = 896
MESH = pl.DeviceIdType.MESH
F32 = jnp.float32
BF16 = jnp.bfloat16
NT = (((1,), (1,)), ((), ()))


def remote(src, dst, send, recv, device):
    return pltpu.make_async_remote_copy(
        src_ref=src, dst_ref=dst, send_sem=send, recv_sem=recv, device_id=device, device_id_type=MESH
    )


def kernel(
    x_hbm, car_hbm, gain_hbm, w_hbm, cot_hbm,
    gi_hbm, gw_hbm, gg_hbm,
    gi_ref, gw_ref, gg_ref, x_ref, car_ref, gain_ref, cv, cf, fr, rb, hb, colh, wv, ws, wt, uf, ut, dk, p, r0, r1, f0, t2, q2, r2, vs, zb, r3,
    gh, gz, gc,
    in_sem, out_sem, halo_s, halo_r, core_s, core_r, s1s, s1r, s2s, s2r, s3s, s3r, ghs, ghr, gzs, gzr, gcs, gcr,
):
    ha = lax.axis_index("ha")
    wa = lax.axis_index("wa")
    col = lax.axis_index("col")
    qy, qx = ha // 4, ha % 4
    up, down = (ha + 15) % 16, (ha + 1) % 16
    left, right = (wa + 15) % 16, (wa + 1) % 16
    other = 1 - col

    barrier = pltpu.get_barrier_semaphore()
    loads = [
        pltpu.make_async_copy(src, dst, in_sem.at[n])
        for n, (src, dst) in enumerate(
            ((cot_hbm, cv), (x_hbm, x_ref), (car_hbm, car_ref), (gain_hbm, gain_ref), (w_hbm, wv))
        )
    ]
    for load in loads:
        load.start()
    pl.semaphore_signal(barrier, inc=1, device_id=(ha, wa, other), device_id_type=MESH)
    for h in (up, down):
        for w in (left, right):
            pl.semaphore_signal(barrier, inc=1, device_id=(h, w, col), device_id_type=MESH)

    def greet(d, _):
        pl.semaphore_signal(barrier, inc=1, device_id=((ha + d) % 16, wa, col), device_id_type=MESH)
        pl.semaphore_signal(barrier, inc=1, device_id=(ha, (wa + d) % 16, col), device_id_type=MESH)
        return 0

    lax.fori_loop(1, 16, greet, 0)

    vs[:, 112:192, :] = jnp.zeros((3, 80, 128), F32)
    t2[24:32, :] = jnp.zeros((8, HALF), F32)

    loads[0].wait()
    cf[...] = cv[...].astype(F32)
    pad4 = jnp.zeros((TP - T, 128), F32)
    for row in range(2):
        for lt in range(24):
            value = jnp.concatenate([cf[pl.ds(2 * lt + row, T, stride=48), :], pad4], axis=0)
            fr[row, lt] = value
            rb[row, lt] = value.astype(BF16)

    pl.semaphore_wait(barrier, 35)

    halos = []

    def halo(src, dst, device):
        n = len(halos)
        copy = remote(src, dst, halo_s.at[n], halo_r.at[n], device)
        copy.start()
        halos.append(copy)

    first_two, last_two = pl.ds(0, 2), pl.ds(22, 2)
    halo(rb.at[0], hb.at[1], (up, wa, col))
    halo(rb.at[1], hb.at[0], (down, wa, col))
    halo(rb.at[:, first_two], colh.at[1, pl.ds(1, 2)], (ha, left, col))
    halo(rb.at[:, last_two], colh.at[0, pl.ds(1, 2)], (ha, right, col))
    halo(rb.at[0, first_two], colh.at[1, 3], (up, left, col))
    halo(rb.at[0, last_two], colh.at[0, 3], (up, right, col))
    halo(rb.at[1, first_two], colh.at[1, 0], (down, left, col))
    halo(rb.at[1, last_two], colh.at[0, 0], (down, right, col))

    for load in loads[1:4]:
        load.wait()
    gain = gain_ref[...]
    pad = jnp.zeros((TP - T, CH), F32)
    x = jnp.concatenate(
        [piece for s in range(S) for piece in (x_ref[:, s * CH : (s + 1) * CH].astype(F32), pad)], axis=0
    )
    scale = lax.rsqrt(jnp.mean(x * x, axis=-1, keepdims=True) + 1e-06)
    normed = x * scale
    act = normed * gain
    sig = 1.0 / (1.0 + jnp.exp(-act))
    activated = (act * sig).astype(BF16).astype(F32).reshape(S, TP, CH)
    for s in range(S):
        uf[s, 0:2, :] = car_ref[:, s * CH : (s + 1) * CH].astype(F32)
        uf[s, 2 : 2 + TP, :] = activated[s]

    m = lax.broadcasted_iota(jnp.int32, (96, CH), 0)
    lane = lax.broadcasted_iota(jnp.int32, (96, CH), 1)
    first = (m >= 24).astype(jnp.int32) + (m >= 48).astype(jnp.int32) + (m >= 72).astype(jnp.int32)
    rest = m - 24 * first
    second = (rest >= 6).astype(jnp.int32) + (rest >= 12).astype(jnp.int32) + (rest >= 18).astype(jnp.int32)
    swapped = 24 * second + 6 * first + (rest - 6 * second)
    u = jnp.concatenate([uf[:, a : a + TP, :].reshape(ROWS, CH).astype(BF16) for a in range(3)], axis=0)
    for k, half in ((2, other), (0, col)):
        for hf, channel in enumerate((m, swapped)):
            sel = (lane == channel + 96 * half).astype(F32).astype(BF16)
            moved = lax.dot_general(sel, u, NT, preferred_element_type=F32).astype(BF16)
            for a in range(3):
                ut[k, hf, a] = moved[:, a * ROWS : (a + 1) * ROWS]
        if k == 2:
            u_copy = remote(ut.at[2], ut.at[1], core_s.at[0], core_r.at[0], (ha, wa, other))
            u_copy.start()

    for copy in halos:
        copy.wait_recv()
    top = (ha > 0).astype(F32)
    bottom = (ha < 15).astype(F32)
    at_left = (wa > 0).astype(F32)
    at_right = (wa < 15).astype(F32)
    low_lanes = lax.broadcasted_iota(jnp.int32, (TP, 128), 1) < 64

    def turn(tile):
        return pltpu.roll(tile, 64, axis=1)

    def row_sum(b, load):
        one, two = load(b)
        if b == 0:
            two = two * bottom
        if b == 2:
            one = one * top
        return one + two

    def own_rows(lt):
        def load(b):
            if b == 0:
                return fr[1, lt], hb[1, lt].astype(F32)
            if b == 1:
                return fr[0, lt], fr[1, lt]
            return hb[0, lt].astype(F32), fr[0, lt]

        return load

    def side_rows(side, k):
        def load(b):
            return colh[side, 2 - b, k].astype(F32), colh[side, 3 - b, k].astype(F32)

        return load

    columns = {}

    def column(b, j):
        if (b, j) not in columns:
            if j == -1:
                pair = [row_sum(b, side_rows(0, k)) * at_left for k in range(2)]
            elif j == 2 * S:
                pair = [row_sum(b, side_rows(1, k)) * at_right for k in range(2)]
            else:
                pair = [row_sum(b, own_rows(3 * (j // 2) + j % 2 + k)) for k in range(2)]
            turned = [turn(pair[0]), turn(pair[1])]
            if j % 2 == 0:
                moved = [turned[0], jnp.where(low_lanes, turned[0], turned[1])]
            else:
                moved = [jnp.where(low_lanes, turned[0], turned[1]), turned[1]]
            columns[b, j] = (pair, moved)
        return columns[b, j]

    def cells(be, s, k):
        b, e = be // 3, be % 3
        j = 2 * s + 1 - e
        total = None
        for c in (j, j + 1):
            natural, moved = column(b, c)
            tile = natural[k] if c % 2 == be % 2 else moved[k]
            total = tile if total is None else total + tile
        return total

    d_copies = []
    for hf in range(2):
        for s in range(S):
            for n in range(7 * hf, 7 * hf + 7):
                be, k = 2 * (n // 3), n % 3
                if k == 0:
                    tile = cells(be, s, 0)
                elif k == 1:
                    tile = jnp.where(low_lanes, cells(be, s, 1), cells(be + 1, s, 0) if be < 8 else 0.0)
                else:
                    tile = cells(be + 1, s, 1)
                high = tile.astype(BF16)
                low = (tile - high.astype(F32)).astype(BF16)
                dk[s * TP : (s + 1) * TP, n * 128 : (n + 1) * 128] = high
                dk[ROWS + s * TP : ROWS + (s + 1) * TP, n * 128 : (n + 1) * 128] = low
        lanes = pl.ds(hf * HALF, HALF)
        copy = remote(
            dk.at[pl.ds(0, 2 * ROWS), lanes], dk.at[pl.ds(2 * ROWS, 2 * ROWS), lanes],
            core_s.at[1 + hf], core_r.at[1 + hf], (ha, wa, other),
        )
        copy.start()
        d_copies.append(copy)

    loads[4].wait()

    def widen(n, _):
        lanes = pl.ds(pl.multiple_of(n * 128, 128), 128)
        for t8 in range(4):
            count = 8 if t8 < 3 else 3
            at = pl.multiple_of((t8 * 288 + n) * 8, 8)
            ws[pl.ds(at, count), :] = wv[t8 * 8 : t8 * 8 + count, lanes].astype(F32)
        return 0

    lax.fori_loop(0, 288, widen, 0, unroll=8)
    low_wide = lax.broadcasted_iota(jnp.int32, (96, 128), 1) < 64
    for a in range(3):
        for parity in range(2):
            at = a * 256 + parity * 128
            wt[at + 96 : at + 128, :] = jnp.zeros((32, 2 * HALF), BF16)
        even = slice(a * 256, a * 256 + 96)
        odd = slice(a * 256 + 128, a * 256 + 224)
        for k in range(5):

            def tap(be, j):
                t8, tr = (9 * a + be) // 8, (9 * a + be) % 8
                return ws[pl.ds((t8 * 288 + j) * 8 + tr, 96, stride=24), :]

            a0, a1, a2 = (tap(2 * k, j) for j in range(3))
            t1, t2w = turn(a1), turn(a2)
            at = k * 384
            wt[even, at : at + 128] = a0.astype(BF16)
            wt[odd, at : at + 128] = jnp.where(low_wide, t1, t2w).astype(BF16)
            if k < 4:
                b0, b1, b2 = (tap(2 * k + 1, j) for j in range(3))
                s0, s1 = turn(b0), turn(b1)
                wt[even, at + 128 : at + 256] = jnp.where(low_wide, a1, s0).astype(BF16)
                wt[even, at + 256 : at + 384] = jnp.where(low_wide, s0, s1).astype(BF16)
                wt[odd, at + 128 : at + 256] = jnp.where(low_wide, t2w, b1).astype(BF16)
                wt[odd, at + 256 : at + 384] = b2.astype(BF16)
            else:
                wt[even, at + 128 : at + 256] = jnp.where(low_wide, a1, 0.0).astype(BF16)
                wt[odd, at + 128 : at + 256] = jnp.where(low_wide, t2w, 0.0).astype(BF16)

    def ring(hf, d):
        if hf == 0:
            return ((qy + d) % 4) * 4 + qx
        return qy * 4 + (qx + d) % 4

    mine = (qy, qx)
    u_copy.wait_recv()
    ones = {}

    def first_send(key, src, dst, hf, d):
        a = key[0]
        copy = remote(src, dst, s1s.at[a, hf, key[2]], s1r.at[a, hf, key[2]], (ring(hf, d), wa, col))
        copy.start()
        ones[key] = copy

    def cut(a):
        c = 512 if a % 2 == 0 else 384
        return pl.ds(0, c), pl.ds(c, HALF - c)

    for hf in range(2):
        d_copies[hf].wait_recv()
        own, his = (ut[k, hf].reshape(288, ROWS) for k in range(2))
        lhs = jnp.concatenate([own, own, his, his], axis=1)
        part = jnp.dot(lhs, dk[:, hf * HALF : (hf + 1) * HALF], preferred_element_type=F32)
        p[hf] = part.reshape(3, 4, 24, HALF)
        q = mine[hf]
        for a in range(3):
            one, two = cut(a)
            far, near, back = (q + 2) % 4, (q + 1) % 4, (q + 3) % 4
            first_send((a, hf, 0), p.at[hf, a, far, :, one], r0.at[a, hf, :, one], hf, 1)
            first_send((a, hf, 1), p.at[hf, a, far, :, two], r0.at[a, hf, :, two], hf, 3)
            first_send((a, hf, 2), p.at[hf, a, near, :, two], r1.at[a, hf, 0, :, two], hf, 1)
            first_send((a, hf, 3), p.at[hf, a, back, :, one], r1.at[a, hf, 1, :, one], hf, 3)

    def pass_on(a):
        one, two = cut(a)
        for hf in range(2):
            near, back = (mine[hf] + 1) % 4, (mine[hf] + 3) % 4
            ones[a, hf, 0].wait_recv()
            f0[a, hf, :, one] = p[hf, a, near, :, one] + r0[a, hf, :, one]
            first_send((a, hf, 4), f0.at[a, hf, :, one], r1.at[a, hf, 0, :, one], hf, 1)
            ones[a, hf, 1].wait_recv()
            f0[a, hf, :, two] = p[hf, a, back, :, two] + r0[a, hf, :, two]
            first_send((a, hf, 5), f0.at[a, hf, :, two], r1.at[a, hf, 1, :, two], hf, 3)

    g = lax.dot_general(dk[0 : 2 * ROWS, :], wt[...], NT, preferred_element_type=F32)
    pass_on(0)
    g = g[0:ROWS] + g[ROWS : 2 * ROWS]
    g = g[:, 512:768] + pltpu.roll(g[:, 256:512], ROWS - 1, axis=0) + pltpu.roll(g[:, 0:256], ROWS - 2, axis=0)
    k = lax.broadcasted_iota(jnp.int32, (256, CH), 0)
    chan = lax.broadcasted_iota(jnp.int32, (256, CH), 1)
    spread = (chan == jnp.where(k < 128, 2 * k, 2 * (k - 128) + 1)).astype(F32).astype(BF16)
    high = g.astype(BF16)
    low = (g - high.astype(F32)).astype(BF16)
    coarse = jnp.dot(jnp.concatenate([high, low], axis=0), spread, preferred_element_type=F32)
    coarse = coarse[0:ROWS] + coarse[ROWS : 2 * ROWS]
    pass_on(1)
    grad_act = coarse * (sig * (1.0 + act * (1.0 - sig)))
    gain_term = jnp.sum(grad_act * normed, axis=0, keepdims=True)
    gh[ha] = jnp.concatenate([gain_term, jnp.zeros((1, 64), F32)], axis=1)

    def gh_send(d, _):
        remote(gh.at[ha], gh.at[ha], ghs.at[d - 1], ghr.at[d - 1], ((ha + d) % 16, wa, col)).start()
        return 0

    lax.fori_loop(1, 16, gh_send, 0)
    pass_on(2)
    grad_normed = grad_act * gain
    grad_in = scale * (grad_normed - normed * jnp.mean(grad_normed * normed, axis=-1, keepdims=True))
    for s in range(S):
        gi_ref[:, s * CH : (s + 1) * CH] = grad_in[s * TP : s * TP + T].astype(BF16)
    gi_out = pltpu.make_async_copy(gi_ref, gi_hbm, out_sem.at[0])
    gi_out.start()

    twos = {}

    def second(a):
        for hf in range(2):
            for n in range(2, 6):
                ones[a, hf, n].wait_recv()
            t2[0:24, :] = p[hf, a, mine[hf]] + r1[a, hf, 0] + r1[a, hf, 1]
            for k in range(4):
                q2[a, hf, k] = t2[6 * k : 6 * k + 8, :]
            for d in range(1, 4):
                copy = remote(
                    q2.at[a, hf, (mine[1 - hf] + d) % 4], r2.at[a, hf, d - 1], s2s.at[a, hf, d - 1],
                    s2r.at[a, hf, d - 1], (ring(1 - hf, d), wa, col),
                )
                copy.start()
                twos[a, hf, d] = copy

    def third(a):
        for hf in range(2):
            for d in range(1, 4):
                twos[a, hf, d].wait_recv()
            total = q2[a, hf, mine[1 - hf]] + r2[a, hf, 0] + r2[a, hf, 1] + r2[a, hf, 2]
            for k in range(7):
                at = (7 * hf + k) * 8
                vs[a, at : at + 8, :] = total[:, k * 128 : (k + 1) * 128]
        y = []
        for i in range(6):
            tiles = jnp.concatenate([vs[a, pl.ds(j * 8 + i, 8, stride=24), :] for j in range(3)], axis=1)
            y.append((tiles[:, 0:CH], tiles[:, CH : 2 * CH]))
        for w in range(16):
            i0, o0 = (72 * w) // CH, (72 * w) % CH
            n0 = min(72, CH - o0)
            pieces = []
            for parity in range(2):
                pieces.append(y[i0][parity][:, o0 : o0 + n0])
                if n0 < 72:
                    pieces.append(y[i0 + 1][parity][:, 0 : 72 - n0])
            tile = jnp.concatenate(pieces, axis=1)
            zb[a, w] = tile[:, 0:128]
            spare = jnp.concatenate([tile[k : k + 1, 128:144] for k in range(4)], axis=1)
            zb[a, w, 5:6, 0:64] = spare

        def z_send(d, _):
            remote(
                zb.at[a, (wa + d) % 16], r3.at[a, d - 1], s3s.at[a, d - 1], s3r.at[a, d - 1],
                (ha, (wa + d) % 16, col),
            ).start()
            return 0

        lax.fori_loop(1, 16, z_send, 0)

    def finish(a):
        def z_wait(d, _):
            remote(
                zb.at[a, (wa + d) % 16], r3.at[a, d - 1], s3s.at[a, d - 1], s3r.at[a, d - 1],
                (ha, (wa + d) % 16, col),
            ).wait()
            return 0

        lax.fori_loop(1, 16, z_wait, 0)
        total = zb[a, wa] + jnp.sum(r3[a], axis=0)
        for be in range(9):
            k = be // 2
            if be % 2 == 0:
                row = total[k : k + 1, 0:72]
            else:
                row = jnp.concatenate([total[k : k + 1, 72:128], total[5:6, 16 * k : 16 * k + 16]], axis=1)
            gw_ref[9 * a + be] = row

    def gh_wait(d, _):
        src = (ha + 16 - d) % 16
        remote(gh.at[ha], gh.at[src], ghs.at[d - 1], ghr.at[d - 1], (src, wa, col)).wait_recv()
        return 0

    def gz_send(d, _):
        remote(gz.at[wa], gz.at[wa], gzs.at[d - 1], gzr.at[d - 1], (ha, (wa + d) % 16, col)).start()
        return 0

    def gz_wait(d, _):
        src = (wa + 16 - d) % 16
        remote(gz.at[wa], gz.at[src], gzs.at[d - 1], gzr.at[d - 1], (ha, src, col)).wait_recv()
        return 0

    second(0)
    second(1)
    lax.fori_loop(1, 16, gh_wait, 0)
    gz[wa] = jnp.sum(gh[...], axis=0)
    lax.fori_loop(1, 16, gz_send, 0)
    third(0)
    second(2)
    third(1)
    lax.fori_loop(1, 16, gz_wait, 0)
    gc[0] = jnp.sum(gz[...], axis=0)
    gc_copy = remote(gc.at[0], gc.at[1], gcs, gcr, (ha, wa, other))
    gc_copy.start()
    third(2)
    finish(0)
    gc_copy.wait()
    gg_ref[...] = (gc[0] + gc[1])[:, 0:CH]
    gg_out = pltpu.make_async_copy(gg_ref, gg_hbm, out_sem.at[1])
    gg_out.start()
    finish(1)
    finish(2)
    gw_out = pltpu.make_async_copy(gw_ref, gw_hbm, out_sem.at[2])
    gw_out.start()

    for copy in halos + d_copies + [u_copy] + list(ones.values()) + list(twos.values()):
        copy.wait_send()

    def g_done(d, _):
        remote(gh.at[ha], gh.at[ha], ghs.at[d - 1], ghr.at[d - 1], ((ha + d) % 16, wa, col)).wait_send()
        remote(gz.at[wa], gz.at[wa], gzs.at[d - 1], gzr.at[d - 1], (ha, (wa + d) % 16, col)).wait_send()
        return 0

    lax.fori_loop(1, 16, g_done, 0)
    for copy in (gi_out, gg_out, gw_out):
        copy.wait()


def hand_on(gi_from, gw_from, gg_from, gi_to, gw_to, gg_to, sem):
    copies = [
        pltpu.make_async_copy(src, dst, sem.at[n])
        for n, (src, dst) in enumerate(((gi_from, gi_to), (gw_from, gw_to), (gg_from, gg_to)))
    ]
    for copy in copies:
        copy.start()
    for copy in copies:
        copy.wait()


def on_device(inputs, carried, gain, weight, cotangent):
    hbm = pl.BlockSpec(memory_space=pl.ANY)
    dma = pltpu.SemaphoreType.DMA
    outs = (
        jax.ShapeDtypeStruct((T, S * CH), BF16),
        jax.ShapeDtypeStruct((27, 1, 72), F32),
        jax.ShapeDtypeStruct((1, CH), F32),
    )
    results = pl.pallas_call(
        kernel,
        out_shape=outs,
        in_specs=[hbm] * 5,
        out_specs=(hbm, hbm, hbm),
        scratch_shapes=[
            pltpu.VMEM((T, S * CH), BF16),
            pltpu.VMEM((27, 1, 72), F32),
            pltpu.VMEM((1, CH), F32),
            pltpu.VMEM((T, S * CH), BF16),
            pltpu.VMEM((2, S * CH), BF16),
            pltpu.VMEM((1, CH), F32),
            pltpu.VMEM((576, 128), BF16),
            pltpu.VMEM((576, 128), F32),
            pltpu.VMEM((2, 24, TP, 128), F32),
            pltpu.VMEM((2, 24, TP, 128), BF16),
            pltpu.VMEM((2, 24, TP, 128), BF16),
            pltpu.VMEM((2, 4, 2, TP, 128), BF16),
            pltpu.VMEM((27, CH * CH), BF16),
            pltpu.VMEM((4 * 288 * 8, 128), F32),
            pltpu.VMEM((768, 2 * HALF), BF16),
            pltpu.VMEM((S, 24, CH), F32),
            pltpu.VMEM((3, 2, 3, 96, ROWS), BF16),
            pltpu.VMEM((4 * ROWS, 2 * HALF), BF16),
            pltpu.VMEM((2, 3, 4, 24, HALF), F32),
            pltpu.VMEM((3, 2, 24, HALF), F32),
            pltpu.VMEM((3, 2, 2, 24, HALF), F32),
            pltpu.VMEM((3, 2, 24, HALF), F32),
            pltpu.VMEM((32, HALF), F32),
            pltpu.VMEM((3, 2, 4, 8, HALF), F32),
            pltpu.VMEM((3, 2, 3, 8, HALF), F32),
            pltpu.VMEM((3, 192, 128), F32),
            pltpu.VMEM((3, 16, 8, 128), F32),
            pltpu.VMEM((3, 15, 8, 128), F32),
            pltpu.VMEM((16, 1, 256), F32),
            pltpu.VMEM((16, 1, 256), F32),
            pltpu.VMEM((2, 1, 256), F32),
            dma((5,)), dma((3,)), dma((8,)), dma((8,)), dma((3,)), dma((3,)),
            dma((3, 2, 6)), dma((3, 2, 6)), dma((3, 2, 3)), dma((3, 2, 3)),
            dma((3, 15)), dma((3, 15)), dma((15,)), dma((15,)), dma((15,)), dma((15,)), dma(()), dma(()),
        ],
        compiler_params=pltpu.CompilerParams(
            collective_id=0, has_side_effects=True, vmem_limit_bytes=62 * 1024 * 1024
        ),
    )(
        inputs.reshape(T, S * CH),
        carried.reshape(2, S * CH),
        gain.reshape(1, CH),
        weight,
        cotangent.reshape(T, 2, 24, 128).transpose(0, 2, 1, 3).reshape(576, 128),
    )
    gi, gw, gg = pl.pallas_call(
        hand_on, out_shape=outs, in_specs=[hbm] * 3, out_specs=(hbm, hbm, hbm), scratch_shapes=[dma((3,))],
        compiler_params=pltpu.CompilerParams(vmem_limit_bytes=62 * 1024 * 1024),
    )(*results)
    return gi.reshape(inputs.shape), gw.reshape(1, 27, 72), gg.reshape(CH)


def solution(mesh):
    placed = (
        P("col", None, "ha", "wa"),
        P("col", None, "ha", "wa"),
        P(),
        P(),
        P("col", None, "ha", "wa"),
    )
    return jax.shard_map(
        on_device,
        mesh=mesh,
        in_specs=placed,
        out_specs=(P("col", None, "ha", "wa"), P("col", None, ("ha", "wa")), P()),
        check_vma=False,
    )
```

```python
import functools

import jax
import jax.numpy as jnp
from jax import lax
from jax.experimental import pallas as pl
from jax.experimental.pallas import tpu as pltpu
from jax.sharding import PartitionSpec as P

CH = 192
T = 12
S = 8
TP = 16
ROWS = S * TP
HALF = 896
MESH = pl.DeviceIdType.MESH
F32 = jnp.float32
BF16 = jnp.bfloat16
NT = (((1,), (1,)), ((), ()))


def remote(src, dst, send, recv, device):
    return pltpu.make_async_remote_copy(
        src_ref=src, dst_ref=dst, send_sem=send, recv_sem=recv, device_id=device, device_id_type=MESH
    )


def kernel(
    x_hbm, car_hbm, gain_hbm, w_hbm, cot_hbm,
    gi_hbm, gw_hbm, gg_hbm,
    gi_ref, gw_ref, gg_ref, x_ref, car_ref, gain_ref, cv, cf, fr, rb, hb, colh, wv, ws, wt, uf, ut, dk, p, r0, r1, f0, t2, q2, r2, vs, zb, r3,
    gh, gz, gc,
    in_sem, out_sem, halo_s, halo_r, core_s, core_r, s1s, s1r, s2s, s2r, s3s, s3r, ghs, ghr, gzs, gzr, gcs, gcr,
):
    ha = lax.axis_index("ha")
    wa = lax.axis_index("wa")
    col = lax.axis_index("col")
    qy, qx = ha // 4, ha % 4
    up, down = (ha + 15) % 16, (ha + 1) % 16
    left, right = (wa + 15) % 16, (wa + 1) % 16
    other = 1 - col

    barrier = pltpu.get_barrier_semaphore()
    loads = [
        pltpu.make_async_copy(src, dst, in_sem.at[n])
        for n, (src, dst) in enumerate(
            ((cot_hbm, cv), (x_hbm, x_ref), (car_hbm, car_ref), (gain_hbm, gain_ref), (w_hbm, wv))
        )
    ]
    for load in loads:
        load.start()
    pl.semaphore_signal(barrier, inc=1, device_id=(ha, wa, other), device_id_type=MESH)
    for h in (up, down):
        for w in (left, right):
            pl.semaphore_signal(barrier, inc=1, device_id=(h, w, col), device_id_type=MESH)

    def greet(d, _):
        pl.semaphore_signal(barrier, inc=1, device_id=((ha + d) % 16, wa, col), device_id_type=MESH)
        pl.semaphore_signal(barrier, inc=1, device_id=(ha, (wa + d) % 16, col), device_id_type=MESH)
        return 0

    lax.fori_loop(1, 16, greet, 0)

    vs[:, 112:192, :] = jnp.zeros((3, 80, 128), F32)
    t2[24:32, :] = jnp.zeros((8, HALF), F32)

    loads[0].wait()
    cf[...] = cv[...].astype(F32)
    pad4 = jnp.zeros((TP - T, 128), F32)
    for row in range(2):
        for lt in range(24):
            value = jnp.concatenate([cf[pl.ds(2 * lt + row, T, stride=48), :], pad4], axis=0)
            fr[row, lt] = value
            rb[row, lt] = value.astype(BF16)

    pl.semaphore_wait(barrier, 35)

    halos = []

    def halo(src, dst, device):
        n = len(halos)
        copy = remote(src, dst, halo_s.at[n], halo_r.at[n], device)
        copy.start()
        halos.append(copy)

    first_two, last_two = pl.ds(0, 2), pl.ds(22, 2)
    halo(rb.at[0], hb.at[1], (up, wa, col))
    halo(rb.at[1], hb.at[0], (down, wa, col))
    halo(rb.at[:, first_two], colh.at[1, pl.ds(1, 2)], (ha, left, col))
    halo(rb.at[:, last_two], colh.at[0, pl.ds(1, 2)], (ha, right, col))
    halo(rb.at[0, first_two], colh.at[1, 3], (up, left, col))
    halo(rb.at[0, last_two], colh.at[0, 3], (up, right, col))
    halo(rb.at[1, first_two], colh.at[1, 0], (down, left, col))
    halo(rb.at[1, last_two], colh.at[0, 0], (down, right, col))

    for load in loads[1:4]:
        load.wait()
    gain = gain_ref[...]
    pad = jnp.zeros((TP - T, CH), F32)
    x = jnp.concatenate(
        [piece for s in range(S) for piece in (x_ref[:, s * CH : (s + 1) * CH].astype(F32), pad)], axis=0
    )
    scale = lax.rsqrt(jnp.mean(x * x, axis=-1, keepdims=True) + 1e-06)
    normed = x * scale
    act = normed * gain
    sig = 1.0 / (1.0 + jnp.exp(-act))
    activated = (act * sig).astype(BF16).astype(F32).reshape(S, TP, CH)
    for s in range(S):
        uf[s, 0:2, :] = car_ref[:, s * CH : (s + 1) * CH].astype(F32)
        uf[s, 2 : 2 + TP, :] = activated[s]

    m = lax.broadcasted_iota(jnp.int32, (96, CH), 0)
    lane = lax.broadcasted_iota(jnp.int32, (96, CH), 1)
    first = (m >= 24).astype(jnp.int32) + (m >= 48).astype(jnp.int32) + (m >= 72).astype(jnp.int32)
    rest = m - 24 * first
    second = (rest >= 6).astype(jnp.int32) + (rest >= 12).astype(jnp.int32) + (rest >= 18).astype(jnp.int32)
    swapped = 24 * second + 6 * first + (rest - 6 * second)
    u = jnp.concatenate([uf[:, a : a + TP, :].reshape(ROWS, CH).astype(BF16) for a in range(3)], axis=0)
    for k, half in ((2, other), (0, col)):
        for hf, channel in enumerate((m, swapped)):
            sel = (lane == channel + 96 * half).astype(F32).astype(BF16)
            moved = lax.dot_general(sel, u, NT, preferred_element_type=F32).astype(BF16)
            for a in range(3):
                ut[k, hf, a] = moved[:, a * ROWS : (a + 1) * ROWS]
        if k == 2:
            u_copy = remote(ut.at[2], ut.at[1], core_s.at[0], core_r.at[0], (ha, wa, other))
            u_copy.start()

    for copy in halos:
        copy.wait_recv()
    top = (ha > 0).astype(F32)
    bottom = (ha < 15).astype(F32)
    at_left = (wa > 0).astype(F32)
    at_right = (wa < 15).astype(F32)
    low_lanes = lax.broadcasted_iota(jnp.int32, (TP, 128), 1) < 64

    def turn(tile):
        return pltpu.roll(tile, 64, axis=1)

    def row_sum(b, load):
        one, two = load(b)
        if b == 0:
            two = two * bottom
        if b == 2:
            one = one * top
        return one + two

    def own_rows(lt):
        def load(b):
            if b == 0:
                return fr[1, lt], hb[1, lt].astype(F32)
            if b == 1:
                return fr[0, lt], fr[1, lt]
            return hb[0, lt].astype(F32), fr[0, lt]

        return load

    def side_rows(side, k):
        def load(b):
            return colh[side, 2 - b, k].astype(F32), colh[side, 3 - b, k].astype(F32)

        return load

    columns = {}

    def column(b, j):
        if (b, j) not in columns:
            if j == -1:
                pair = [row_sum(b, side_rows(0, k)) * at_left for k in range(2)]
            elif j == 2 * S:
                pair = [row_sum(b, side_rows(1, k)) * at_right for k in range(2)]
            else:
                pair = [row_sum(b, own_rows(3 * (j // 2) + j % 2 + k)) for k in range(2)]
            turned = [turn(pair[0]), turn(pair[1])]
            if j % 2 == 0:
                moved = [turned[0], jnp.where(low_lanes, turned[0], turned[1])]
            else:
                moved = [jnp.where(low_lanes, turned[0], turned[1]), turned[1]]
            columns[b, j] = (pair, moved)
        return columns[b, j]

    def cells(be, s, k):
        b, e = be // 3, be % 3
        j = 2 * s + 1 - e
        total = None
        for c in (j, j + 1):
            natural, moved = column(b, c)
            tile = natural[k] if c % 2 == be % 2 else moved[k]
            total = tile if total is None else total + tile
        return total

    d_copies = []
    for hf in range(2):
        for s in range(S):
            for n in range(7 * hf, 7 * hf + 7):
                be, k = 2 * (n // 3), n % 3
                if k == 0:
                    tile = cells(be, s, 0)
                elif k == 1:
                    tile = jnp.where(low_lanes, cells(be, s, 1), cells(be + 1, s, 0) if be < 8 else 0.0)
                else:
                    tile = cells(be + 1, s, 1)
                high = tile.astype(BF16)
                low = (tile - high.astype(F32)).astype(BF16)
                dk[s * TP : (s + 1) * TP, n * 128 : (n + 1) * 128] = high
                dk[ROWS + s * TP : ROWS + (s + 1) * TP, n * 128 : (n + 1) * 128] = low
        lanes = pl.ds(hf * HALF, HALF)
        copy = remote(
            dk.at[pl.ds(0, 2 * ROWS), lanes], dk.at[pl.ds(2 * ROWS, 2 * ROWS), lanes],
            core_s.at[1 + hf], core_r.at[1 + hf], (ha, wa, other),
        )
        copy.start()
        d_copies.append(copy)

    loads[4].wait()

    def widen(n, _):
        lanes = pl.ds(pl.multiple_of(n * 128, 128), 128)
        for t8 in range(4):
            count = 8 if t8 < 3 else 3
            at = pl.multiple_of((t8 * 288 + n) * 8, 8)
            ws[pl.ds(at, count), :] = wv[t8 * 8 : t8 * 8 + count, lanes].astype(F32)
        return 0

    lax.fori_loop(0, 288, widen, 0, unroll=8)
    low_wide = lax.broadcasted_iota(jnp.int32, (96, 128), 1) < 64
    for a in range(3):
        for parity in range(2):
            at = a * 256 + parity * 128
            wt[at + 96 : at + 128, :] = jnp.zeros((32, 2 * HALF), BF16)
        even = slice(a * 256, a * 256 + 96)
        odd = slice(a * 256 + 128, a * 256 + 224)
        for k in range(5):

            def tap(be, j):
                t8, tr = (9 * a + be) // 8, (9 * a + be) % 8
                return ws[pl.ds((t8 * 288 + j) * 8 + tr, 96, stride=24), :]

            a0, a1, a2 = (tap(2 * k, j) for j in range(3))
            t1, t2w = turn(a1), turn(a2)
            at = k * 384
            wt[even, at : at + 128] = a0.astype(BF16)
            wt[odd, at : at + 128] = jnp.where(low_wide, t1, t2w).astype(BF16)
            if k < 4:
                b0, b1, b2 = (tap(2 * k + 1, j) for j in range(3))
                s0, s1 = turn(b0), turn(b1)
                wt[even, at + 128 : at + 256] = jnp.where(low_wide, a1, s0).astype(BF16)
                wt[even, at + 256 : at + 384] = jnp.where(low_wide, s0, s1).astype(BF16)
                wt[odd, at + 128 : at + 256] = jnp.where(low_wide, t2w, b1).astype(BF16)
                wt[odd, at + 256 : at + 384] = b2.astype(BF16)
            else:
                wt[even, at + 128 : at + 256] = jnp.where(low_wide, a1, 0.0).astype(BF16)
                wt[odd, at + 128 : at + 256] = jnp.where(low_wide, t2w, 0.0).astype(BF16)

    def ring(hf, d):
        if hf == 0:
            return ((qy + d) % 4) * 4 + qx
        return qy * 4 + (qx + d) % 4

    mine = (qy, qx)
    u_copy.wait_recv()
    ones = {}

    def first_send(key, src, dst, hf, d):
        a = key[0]
        copy = remote(src, dst, s1s.at[a, hf, key[2]], s1r.at[a, hf, key[2]], (ring(hf, d), wa, col))
        copy.start()
        ones[key] = copy

    def cut(a):
        c = 512 if a % 2 == 0 else 384
        return pl.ds(0, c), pl.ds(c, HALF - c)

    def first(a, hf):
        q = mine[hf]
        one, two = cut(a)
        far, near, back = (q + 2) % 4, (q + 1) % 4, (q + 3) % 4
        first_send((a, hf, 0), p.at[hf, a, far, :, one], r0.at[a, hf, :, one], hf, 1)
        first_send((a, hf, 1), p.at[hf, a, far, :, two], r0.at[a, hf, :, two], hf, 3)
        first_send((a, hf, 2), p.at[hf, a, near, :, two], r1.at[a, hf, 0, :, two], hf, 1)
        first_send((a, hf, 3), p.at[hf, a, back, :, one], r1.at[a, hf, 1, :, one], hf, 3)

    for hf in range(2):
        d_copies[hf].wait_recv()
        own, his = (ut[k, hf].reshape(288, ROWS) for k in range(2))
        lhs = jnp.concatenate([own, own, his, his], axis=1)
        part = jnp.dot(lhs, dk[:, hf * HALF : (hf + 1) * HALF], preferred_element_type=F32)
        p[hf] = part.reshape(3, 4, 24, HALF)
        if hf == 0:
            first(0, 0)
    first(0, 1)
    first(1, 0)
    first(1, 1)

    def pass_on(a):
        one, two = cut(a)
        for hf in range(2):
            near, back = (mine[hf] + 1) % 4, (mine[hf] + 3) % 4
            ones[a, hf, 0].wait_recv()
            f0[a, hf, :, one] = p[hf, a, near, :, one] + r0[a, hf, :, one]
            first_send((a, hf, 4), f0.at[a, hf, :, one], r1.at[a, hf, 0, :, one], hf, 1)
            ones[a, hf, 1].wait_recv()
            f0[a, hf, :, two] = p[hf, a, back, :, two] + r0[a, hf, :, two]
            first_send((a, hf, 5), f0.at[a, hf, :, two], r1.at[a, hf, 1, :, two], hf, 3)

    twos = {}

    def second(a):
        for hf in range(2):
            for n in range(2, 6):
                ones[a, hf, n].wait_recv()
            t2[0:24, :] = p[hf, a, mine[hf]] + r1[a, hf, 0] + r1[a, hf, 1]
            for k in range(4):
                q2[a, hf, k] = t2[6 * k : 6 * k + 8, :]
            for d in range(1, 4):
                copy = remote(
                    q2.at[a, hf, (mine[1 - hf] + d) % 4], r2.at[a, hf, d - 1], s2s.at[a, hf, d - 1],
                    s2r.at[a, hf, d - 1], (ring(1 - hf, d), wa, col),
                )
                copy.start()
                twos[a, hf, d] = copy

    def third(a):
        for hf in range(2):
            for d in range(1, 4):
                twos[a, hf, d].wait_recv()
            total = q2[a, hf, mine[1 - hf]] + r2[a, hf, 0] + r2[a, hf, 1] + r2[a, hf, 2]
            for k in range(7):
                at = (7 * hf + k) * 8
                vs[a, at : at + 8, :] = total[:, k * 128 : (k + 1) * 128]
        y = []
        for i in range(6):
            tiles = jnp.concatenate([vs[a, pl.ds(j * 8 + i, 8, stride=24), :] for j in range(3)], axis=1)
            y.append((tiles[:, 0:CH], tiles[:, CH : 2 * CH]))
        for w in range(16):
            i0, o0 = (72 * w) // CH, (72 * w) % CH
            n0 = min(72, CH - o0)
            pieces = []
            for parity in range(2):
                pieces.append(y[i0][parity][:, o0 : o0 + n0])
                if n0 < 72:
                    pieces.append(y[i0 + 1][parity][:, 0 : 72 - n0])
            tile = jnp.concatenate(pieces, axis=1)
            zb[a, w] = tile[:, 0:128]
            spare = jnp.concatenate([tile[k : k + 1, 128:144] for k in range(4)], axis=1)
            zb[a, w, 5:6, 0:64] = spare

        def z_send(d, _):
            remote(
                zb.at[a, (wa + d) % 16], r3.at[a, d - 1], s3s.at[a, d - 1], s3r.at[a, d - 1],
                (ha, (wa + d) % 16, col),
            ).start()
            return 0

        lax.fori_loop(1, 16, z_send, 0)

    def finish(a):
        def z_wait(d, _):
            remote(
                zb.at[a, (wa + d) % 16], r3.at[a, d - 1], s3s.at[a, d - 1], s3r.at[a, d - 1],
                (ha, (wa + d) % 16, col),
            ).wait()
            return 0

        lax.fori_loop(1, 16, z_wait, 0)
        total = zb[a, wa] + jnp.sum(r3[a], axis=0)
        for be in range(9):
            k = be // 2
            if be % 2 == 0:
                row = total[k : k + 1, 0:72]
            else:
                row = jnp.concatenate([total[k : k + 1, 72:128], total[5:6, 16 * k : 16 * k + 16]], axis=1)
            gw_ref[9 * a + be] = row

    def gh_wait(d, _):
        src = (ha + 16 - d) % 16
        remote(gh.at[ha], gh.at[src], ghs.at[d - 1], ghr.at[d - 1], (src, wa, col)).wait_recv()
        return 0

    def gz_send(d, _):
        remote(gz.at[wa], gz.at[wa], gzs.at[d - 1], gzr.at[d - 1], (ha, (wa + d) % 16, col)).start()
        return 0

    def gz_wait(d, _):
        src = (wa + 16 - d) % 16
        remote(gz.at[wa], gz.at[src], gzs.at[d - 1], gzr.at[d - 1], (ha, src, col)).wait_recv()
        return 0

    g = lax.dot_general(dk[0 : 2 * ROWS, :], wt[...], NT, preferred_element_type=F32)
    pass_on(0)
    first(2, 0)
    first(2, 1)
    g = g[0:ROWS] + g[ROWS : 2 * ROWS]
    g = g[:, 512:768] + pltpu.roll(g[:, 256:512], ROWS - 1, axis=0) + pltpu.roll(g[:, 0:256], ROWS - 2, axis=0)
    k = lax.broadcasted_iota(jnp.int32, (256, CH), 0)
    chan = lax.broadcasted_iota(jnp.int32, (256, CH), 1)
    spread = (chan == jnp.where(k < 128, 2 * k, 2 * (k - 128) + 1)).astype(F32).astype(BF16)
    high = g.astype(BF16)
    low = (g - high.astype(F32)).astype(BF16)
    coarse = jnp.dot(jnp.concatenate([high, low], axis=0), spread, preferred_element_type=F32)
    coarse = coarse[0:ROWS] + coarse[ROWS : 2 * ROWS]
    pass_on(1)
    second(0)
    grad_act = coarse * (sig * (1.0 + act * (1.0 - sig)))
    gain_term = jnp.sum(grad_act * normed, axis=0, keepdims=True)
    gh[ha] = jnp.concatenate([gain_term, jnp.zeros((1, 64), F32)], axis=1)

    def gh_send(d, _):
        remote(gh.at[ha], gh.at[ha], ghs.at[d - 1], ghr.at[d - 1], ((ha + d) % 16, wa, col)).start()
        return 0

    lax.fori_loop(1, 16, gh_send, 0)
    second(1)
    third(0)
    pass_on(2)
    grad_normed = grad_act * gain
    grad_in = scale * (grad_normed - normed * jnp.mean(grad_normed * normed, axis=-1, keepdims=True))
    for s in range(S):
        gi_ref[:, s * CH : (s + 1) * CH] = grad_in[s * TP : s * TP + T].astype(BF16)
    gi_out = pltpu.make_async_copy(gi_ref, gi_hbm, out_sem.at[0])
    gi_out.start()

    third(1)
    second(2)
    lax.fori_loop(1, 16, gh_wait, 0)
    gz[wa] = jnp.sum(gh[...], axis=0)
    lax.fori_loop(1, 16, gz_send, 0)
    third(2)
    finish(0)
    lax.fori_loop(1, 16, gz_wait, 0)
    gc[0] = jnp.sum(gz[...], axis=0)
    gc_copy = remote(gc.at[0], gc.at[1], gcs, gcr, (ha, wa, other))
    gc_copy.start()
    finish(1)
    gc_copy.wait()
    gg_ref[...] = (gc[0] + gc[1])[:, 0:CH]
    gg_out = pltpu.make_async_copy(gg_ref, gg_hbm, out_sem.at[1])
    gg_out.start()
    finish(2)
    gw_out = pltpu.make_async_copy(gw_ref, gw_hbm, out_sem.at[2])
    gw_out.start()

    for copy in halos + d_copies + [u_copy] + list(ones.values()) + list(twos.values()):
        copy.wait_send()

    def g_done(d, _):
        remote(gh.at[ha], gh.at[ha], ghs.at[d - 1], ghr.at[d - 1], ((ha + d) % 16, wa, col)).wait_send()
        remote(gz.at[wa], gz.at[wa], gzs.at[d - 1], gzr.at[d - 1], (ha, (wa + d) % 16, col)).wait_send()
        return 0

    lax.fori_loop(1, 16, g_done, 0)
    for copy in (gi_out, gg_out, gw_out):
        copy.wait()


def hand_on(gi_from, gw_from, gg_from, gi_to, gw_to, gg_to, sem):
    copies = [
        pltpu.make_async_copy(src, dst, sem.at[n])
        for n, (src, dst) in enumerate(((gi_from, gi_to), (gw_from, gw_to), (gg_from, gg_to)))
    ]
    for copy in copies:
        copy.start()
    for copy in copies:
        copy.wait()


def on_device(inputs, carried, gain, weight, cotangent):
    hbm = pl.BlockSpec(memory_space=pl.ANY)
    dma = pltpu.SemaphoreType.DMA
    outs = (
        jax.ShapeDtypeStruct((T, S * CH), BF16),
        jax.ShapeDtypeStruct((27, 1, 72), F32),
        jax.ShapeDtypeStruct((1, CH), F32),
    )
    results = pl.pallas_call(
        kernel,
        out_shape=outs,
        in_specs=[hbm] * 5,
        out_specs=(hbm, hbm, hbm),
        scratch_shapes=[
            pltpu.VMEM((T, S * CH), BF16),
            pltpu.VMEM((27, 1, 72), F32),
            pltpu.VMEM((1, CH), F32),
            pltpu.VMEM((T, S * CH), BF16),
            pltpu.VMEM((2, S * CH), BF16),
            pltpu.VMEM((1, CH), F32),
            pltpu.VMEM((576, 128), BF16),
            pltpu.VMEM((576, 128), F32),
            pltpu.VMEM((2, 24, TP, 128), F32),
            pltpu.VMEM((2, 24, TP, 128), BF16),
            pltpu.VMEM((2, 24, TP, 128), BF16),
            pltpu.VMEM((2, 4, 2, TP, 128), BF16),
            pltpu.VMEM((27, CH * CH), BF16),
            pltpu.VMEM((4 * 288 * 8, 128), F32),
            pltpu.VMEM((768, 2 * HALF), BF16),
            pltpu.VMEM((S, 24, CH), F32),
            pltpu.VMEM((3, 2, 3, 96, ROWS), BF16),
            pltpu.VMEM((4 * ROWS, 2 * HALF), BF16),
            pltpu.VMEM((2, 3, 4, 24, HALF), F32),
            pltpu.VMEM((3, 2, 24, HALF), F32),
            pltpu.VMEM((3, 2, 2, 24, HALF), F32),
            pltpu.VMEM((3, 2, 24, HALF), F32),
            pltpu.VMEM((32, HALF), F32),
            pltpu.VMEM((3, 2, 4, 8, HALF), F32),
            pltpu.VMEM((3, 2, 3, 8, HALF), F32),
            pltpu.VMEM((3, 192, 128), F32),
            pltpu.VMEM((3, 16, 8, 128), F32),
            pltpu.VMEM((3, 15, 8, 128), F32),
            pltpu.VMEM((16, 1, 256), F32),
            pltpu.VMEM((16, 1, 256), F32),
            pltpu.VMEM((2, 1, 256), F32),
            dma((5,)), dma((3,)), dma((8,)), dma((8,)), dma((3,)), dma((3,)),
            dma((3, 2, 6)), dma((3, 2, 6)), dma((3, 2, 3)), dma((3, 2, 3)),
            dma((3, 15)), dma((3, 15)), dma((15,)), dma((15,)), dma((15,)), dma((15,)), dma(()), dma(()),
        ],
        compiler_params=pltpu.CompilerParams(
            collective_id=0, has_side_effects=True, vmem_limit_bytes=62 * 1024 * 1024
        ),
    )(
        inputs.reshape(T, S * CH),
        carried.reshape(2, S * CH),
        gain.reshape(1, CH),
        weight,
        cotangent.reshape(T, 2, 24, 128).transpose(0, 2, 1, 3).reshape(576, 128),
    )
    gi, gw, gg = pl.pallas_call(
        hand_on, out_shape=outs, in_specs=[hbm] * 3, out_specs=(hbm, hbm, hbm), scratch_shapes=[dma((3,))],
        compiler_params=pltpu.CompilerParams(vmem_limit_bytes=62 * 1024 * 1024),
    )(*results)
    return gi.reshape(inputs.shape), gw.reshape(1, 27, 72), gg.reshape(CH)


def solution(mesh):
    placed = (
        P("col", None, "ha", "wa"),
        P("col", None, "ha", "wa"),
        P(),
        P(),
        P("col", None, "ha", "wa"),
    )
    return jax.shard_map(
        on_device,
        mesh=mesh,
        in_specs=placed,
        out_specs=(P("col", None, "ha", "wa"), P("col", None, ("ha", "wa")), P()),
        check_vma=False,
    )
```

```python
import functools

import jax
import jax.numpy as jnp
from jax import lax
from jax.experimental import pallas as pl
from jax.experimental.pallas import tpu as pltpu
from jax.sharding import PartitionSpec as P

CH = 192
T = 12
S = 8
TP = 16
ROWS = S * TP
HALF = 896
MESH = pl.DeviceIdType.MESH
F32 = jnp.float32
BF16 = jnp.bfloat16
NT = (((1,), (1,)), ((), ()))


def remote(src, dst, send, recv, device):
    return pltpu.make_async_remote_copy(
        src_ref=src, dst_ref=dst, send_sem=send, recv_sem=recv, device_id=device, device_id_type=MESH
    )


def kernel(
    x_hbm, car_hbm, gain_hbm, w_hbm, cot_hbm,
    gi_hbm, gw_hbm, gg_hbm,
    gi_ref, gw_ref, gg_ref, x_ref, car_ref, gain_ref, cv, cf, fr, rb, hb, colh, wv, ws, wt, uf, ut, dk, p, r0, r1, f0, t2, q2, r2, vs, zb, r3,
    gh, gz, gc,
    in_sem, out_sem, halo_s, halo_r, core_s, core_r, s1s, s1r, s2s, s2r, s3s, s3r, ghs, ghr, gzs, gzr, gcs, gcr,
):
    ha = lax.axis_index("ha")
    wa = lax.axis_index("wa")
    col = lax.axis_index("col")
    qy, qx = ha // 4, ha % 4
    up, down = (ha + 15) % 16, (ha + 1) % 16
    left, right = (wa + 15) % 16, (wa + 1) % 16
    other = 1 - col

    barrier = pltpu.get_barrier_semaphore()
    loads = [
        pltpu.make_async_copy(src, dst, in_sem.at[n])
        for n, (src, dst) in enumerate(
            ((cot_hbm, cv), (x_hbm, x_ref), (car_hbm, car_ref), (gain_hbm, gain_ref), (w_hbm, wv))
        )
    ]
    for load in loads:
        load.start()
    pl.semaphore_signal(barrier, inc=1, device_id=(ha, wa, other), device_id_type=MESH)
    for h in (up, down):
        for w in (left, right):
            pl.semaphore_signal(barrier, inc=1, device_id=(h, w, col), device_id_type=MESH)

    def greet(d, _):
        pl.semaphore_signal(barrier, inc=1, device_id=((ha + d) % 16, wa, col), device_id_type=MESH)
        pl.semaphore_signal(barrier, inc=1, device_id=(ha, (wa + d) % 16, col), device_id_type=MESH)
        return 0

    lax.fori_loop(1, 16, greet, 0)

    vs[:, 112:192, :] = jnp.zeros((3, 80, 128), F32)
    t2[24:32, :] = jnp.zeros((8, HALF), F32)

    loads[0].wait()
    cf[...] = cv[...].astype(F32)
    pad4 = jnp.zeros((TP - T, 128), F32)
    for row in range(2):
        for lt in range(24):
            value = jnp.concatenate([cf[pl.ds(2 * lt + row, T, stride=48), :], pad4], axis=0)
            fr[row, lt] = value
            rb[row, lt] = value.astype(BF16)

    pl.semaphore_wait(barrier, 35)

    halos = []

    def halo(src, dst, device):
        n = len(halos)
        copy = remote(src, dst, halo_s.at[n], halo_r.at[n], device)
        copy.start()
        halos.append(copy)

    first_two, last_two = pl.ds(0, 2), pl.ds(22, 2)
    halo(rb.at[0], hb.at[1], (up, wa, col))
    halo(rb.at[1], hb.at[0], (down, wa, col))
    halo(rb.at[:, first_two], colh.at[1, pl.ds(1, 2)], (ha, left, col))
    halo(rb.at[:, last_two], colh.at[0, pl.ds(1, 2)], (ha, right, col))
    halo(rb.at[0, first_two], colh.at[1, 3], (up, left, col))
    halo(rb.at[0, last_two], colh.at[0, 3], (up, right, col))
    halo(rb.at[1, first_two], colh.at[1, 0], (down, left, col))
    halo(rb.at[1, last_two], colh.at[0, 0], (down, right, col))

    for load in loads[1:4]:
        load.wait()
    gain = gain_ref[...]
    pad = jnp.zeros((TP - T, CH), F32)
    x = jnp.concatenate(
        [piece for s in range(S) for piece in (x_ref[:, s * CH : (s + 1) * CH].astype(F32), pad)], axis=0
    )
    scale = lax.rsqrt(jnp.mean(x * x, axis=-1, keepdims=True) + 1e-06)
    normed = x * scale
    act = normed * gain
    sig = 1.0 / (1.0 + jnp.exp(-act))
    activated = (act * sig).astype(BF16).astype(F32).reshape(S, TP, CH)
    for s in range(S):
        uf[s, 0:2, :] = car_ref[:, s * CH : (s + 1) * CH].astype(F32)
        uf[s, 2 : 2 + TP, :] = activated[s]

    m = lax.broadcasted_iota(jnp.int32, (96, CH), 0)
    lane = lax.broadcasted_iota(jnp.int32, (96, CH), 1)
    first = (m >= 24).astype(jnp.int32) + (m >= 48).astype(jnp.int32) + (m >= 72).astype(jnp.int32)
    rest = m - 24 * first
    second = (rest >= 6).astype(jnp.int32) + (rest >= 12).astype(jnp.int32) + (rest >= 18).astype(jnp.int32)
    swapped = 24 * second + 6 * first + (rest - 6 * second)
    u = jnp.concatenate([uf[:, a : a + TP, :].reshape(ROWS, CH).astype(BF16) for a in range(3)], axis=0)
    for k, half in ((2, other), (0, col)):
        for hf, channel in enumerate((m, swapped)):
            sel = (lane == channel + 96 * half).astype(F32).astype(BF16)
            moved = lax.dot_general(sel, u, NT, preferred_element_type=F32).astype(BF16)
            for a in range(3):
                ut[k, hf, a] = moved[:, a * ROWS : (a + 1) * ROWS]
        if k == 2:
            u_copy = remote(ut.at[2], ut.at[1], core_s.at[0], core_r.at[0], (ha, wa, other))
            u_copy.start()

    for copy in halos:
        copy.wait_recv()
    top = (ha > 0).astype(F32)
    bottom = (ha < 15).astype(F32)
    at_left = (wa > 0).astype(F32)
    at_right = (wa < 15).astype(F32)
    low_lanes = lax.broadcasted_iota(jnp.int32, (TP, 128), 1) < 64

    def turn(tile):
        return pltpu.roll(tile, 64, axis=1)

    def row_sum(b, load):
        one, two = load(b)
        if b == 0:
            two = two * bottom
        if b == 2:
            one = one * top
        return one + two

    def own_rows(lt):
        def load(b):
            if b == 0:
                return fr[1, lt], hb[1, lt].astype(F32)
            if b == 1:
                return fr[0, lt], fr[1, lt]
            return hb[0, lt].astype(F32), fr[0, lt]

        return load

    def side_rows(side, k):
        def load(b):
            return colh[side, 2 - b, k].astype(F32), colh[side, 3 - b, k].astype(F32)

        return load

    columns = {}

    def column(b, j):
        if (b, j) not in columns:
            if j == -1:
                pair = [row_sum(b, side_rows(0, k)) * at_left for k in range(2)]
            elif j == 2 * S:
                pair = [row_sum(b, side_rows(1, k)) * at_right for k in range(2)]
            else:
                pair = [row_sum(b, own_rows(3 * (j // 2) + j % 2 + k)) for k in range(2)]
            turned = [turn(pair[0]), turn(pair[1])]
            if j % 2 == 0:
                moved = [turned[0], jnp.where(low_lanes, turned[0], turned[1])]
            else:
                moved = [jnp.where(low_lanes, turned[0], turned[1]), turned[1]]
            columns[b, j] = (pair, moved)
        return columns[b, j]

    def cells(be, s, k):
        b, e = be // 3, be % 3
        j = 2 * s + 1 - e
        total = None
        for c in (j, j + 1):
            natural, moved = column(b, c)
            tile = natural[k] if c % 2 == be % 2 else moved[k]
            total = tile if total is None else total + tile
        return total

    d_copies = []
    for hf in range(2):
        for s in range(S):
            for n in range(7 * hf, 7 * hf + 7):
                be, k = 2 * (n // 3), n % 3
                if k == 0:
                    tile = cells(be, s, 0)
                elif k == 1:
                    tile = jnp.where(low_lanes, cells(be, s, 1), cells(be + 1, s, 0) if be < 8 else 0.0)
                else:
                    tile = cells(be + 1, s, 1)
                high = tile.astype(BF16)
                low = (tile - high.astype(F32)).astype(BF16)
                dk[s * TP : (s + 1) * TP, n * 128 : (n + 1) * 128] = high
                dk[ROWS + s * TP : ROWS + (s + 1) * TP, n * 128 : (n + 1) * 128] = low
        lanes = pl.ds(hf * HALF, HALF)
        copy = remote(
            dk.at[pl.ds(0, 2 * ROWS), lanes], dk.at[pl.ds(2 * ROWS, 2 * ROWS), lanes],
            core_s.at[1 + hf], core_r.at[1 + hf], (ha, wa, other),
        )
        copy.start()
        d_copies.append(copy)

    loads[4].wait()

    def widen(n, _):
        lanes = pl.ds(pl.multiple_of(n * 128, 128), 128)
        for t8 in range(4):
            count = 8 if t8 < 3 else 3
            at = pl.multiple_of((t8 * 288 + n) * 8, 8)
            ws[pl.ds(at, count), :] = wv[t8 * 8 : t8 * 8 + count, lanes].astype(F32)
        return 0

    lax.fori_loop(0, 288, widen, 0, unroll=8)
    low_wide = lax.broadcasted_iota(jnp.int32, (96, 128), 1) < 64
    for a in range(3):
        for parity in range(2):
            at = a * 256 + parity * 128
            wt[at + 96 : at + 128, :] = jnp.zeros((32, 2 * HALF), BF16)
        even = slice(a * 256, a * 256 + 96)
        odd = slice(a * 256 + 128, a * 256 + 224)
        for k in range(5):

            def tap(be, j):
                t8, tr = (9 * a + be) // 8, (9 * a + be) % 8
                return ws[pl.ds((t8 * 288 + j) * 8 + tr, 96, stride=24), :]

            a0, a1, a2 = (tap(2 * k, j) for j in range(3))
            t1, t2w = turn(a1), turn(a2)
            at = k * 384
            wt[even, at : at + 128] = a0.astype(BF16)
            wt[odd, at : at + 128] = jnp.where(low_wide, t1, t2w).astype(BF16)
            if k < 4:
                b0, b1, b2 = (tap(2 * k + 1, j) for j in range(3))
                s0, s1 = turn(b0), turn(b1)
                wt[even, at + 128 : at + 256] = jnp.where(low_wide, a1, s0).astype(BF16)
                wt[even, at + 256 : at + 384] = jnp.where(low_wide, s0, s1).astype(BF16)
                wt[odd, at + 128 : at + 256] = jnp.where(low_wide, t2w, b1).astype(BF16)
                wt[odd, at + 256 : at + 384] = b2.astype(BF16)
            else:
                wt[even, at + 128 : at + 256] = jnp.where(low_wide, a1, 0.0).astype(BF16)
                wt[odd, at + 128 : at + 256] = jnp.where(low_wide, t2w, 0.0).astype(BF16)

    def ring(hf, d):
        if hf == 0:
            return ((qy + d) % 4) * 4 + qx
        return qy * 4 + (qx + d) % 4

    mine = (qy, qx)
    u_copy.wait_recv()
    ones = {}

    def first_send(key, src, dst, hf, d):
        a = key[0]
        copy = remote(src, dst, s1s.at[a, hf, key[2]], s1r.at[a, hf, key[2]], (ring(hf, d), wa, col))
        copy.start()
        ones[key] = copy

    def cut(a):
        c = 512 if a % 2 == 0 else 384
        return pl.ds(0, c), pl.ds(c, HALF - c)

    for hf in range(2):
        d_copies[hf].wait_recv()
        own, his = (ut[k, hf].reshape(288, ROWS) for k in range(2))
        lhs = jnp.concatenate([own, own, his, his], axis=1)
        part = jnp.dot(lhs, dk[:, hf * HALF : (hf + 1) * HALF], preferred_element_type=F32)
        p[hf] = part.reshape(3, 4, 24, HALF)
        q = mine[hf]
        for a in range(3):
            one, two = cut(a)
            far, near, back = (q + 2) % 4, (q + 1) % 4, (q + 3) % 4
            first_send((a, hf, 0), p.at[hf, a, far, :, one], r0.at[a, hf, :, one], hf, 1)
            first_send((a, hf, 1), p.at[hf, a, far, :, two], r0.at[a, hf, :, two], hf, 3)
            first_send((a, hf, 2), p.at[hf, a, near, :, two], r1.at[a, hf, 0, :, two], hf, 1)
            first_send((a, hf, 3), p.at[hf, a, back, :, one], r1.at[a, hf, 1, :, one], hf, 3)

    def pass_on(a):
        one, two = cut(a)
        for hf in range(2):
            near, back = (mine[hf] + 1) % 4, (mine[hf] + 3) % 4
            ones[a, hf, 0].wait_recv()
            f0[a, hf, :, one] = p[hf, a, near, :, one] + r0[a, hf, :, one]
            first_send((a, hf, 4), f0.at[a, hf, :, one], r1.at[a, hf, 0, :, one], hf, 1)
            ones[a, hf, 1].wait_recv()
            f0[a, hf, :, two] = p[hf, a, back, :, two] + r0[a, hf, :, two]
            first_send((a, hf, 5), f0.at[a, hf, :, two], r1.at[a, hf, 1, :, two], hf, 3)

    g = lax.dot_general(dk[0 : 2 * ROWS, :], wt[...], NT, preferred_element_type=F32)
    pass_on(0)
    g = g[0:ROWS] + g[ROWS : 2 * ROWS]
    g = g[:, 512:768] + pltpu.roll(g[:, 256:512], ROWS - 1, axis=0) + pltpu.roll(g[:, 0:256], ROWS - 2, axis=0)
    k = lax.broadcasted_iota(jnp.int32, (256, CH), 0)
    chan = lax.broadcasted_iota(jnp.int32, (256, CH), 1)
    spread = (chan == jnp.where(k < 128, 2 * k, 2 * (k - 128) + 1)).astype(F32).astype(BF16)
    high = g.astype(BF16)
    low = (g - high.astype(F32)).astype(BF16)
    coarse = jnp.dot(jnp.concatenate([high, low], axis=0), spread, preferred_element_type=F32)
    coarse = coarse[0:ROWS] + coarse[ROWS : 2 * ROWS]
    pass_on(1)
    grad_act = coarse * (sig * (1.0 + act * (1.0 - sig)))
    gain_term = jnp.sum(grad_act * normed, axis=0, keepdims=True)
    gh[ha] = jnp.concatenate([gain_term, jnp.zeros((1, 64), F32)], axis=1)

    def gh_send(d, _):
        remote(gh.at[ha], gh.at[ha], ghs.at[d - 1], ghr.at[d - 1], ((ha + d) % 16, wa, col)).start()
        return 0

    lax.fori_loop(1, 16, gh_send, 0)
    pass_on(2)
    grad_normed = grad_act * gain
    grad_in = scale * (grad_normed - normed * jnp.mean(grad_normed * normed, axis=-1, keepdims=True))
    for s in range(S):
        gi_ref[:, s * CH : (s + 1) * CH] = grad_in[s * TP : s * TP + T].astype(BF16)
    gi_out = pltpu.make_async_copy(gi_ref, gi_hbm, out_sem.at[0])
    gi_out.start()

    twos = {}

    def second(a):
        for hf in range(2):
            for n in range(2, 6):
                ones[a, hf, n].wait_recv()
            t2[0:24, :] = p[hf, a, mine[hf]] + r1[a, hf, 0] + r1[a, hf, 1]
            for k in range(4):
                q2[a, hf, k] = t2[6 * k : 6 * k + 8, :]
            for d in range(1, 4):
                copy = remote(
                    q2.at[a, hf, (mine[1 - hf] + d) % 4], r2.at[a, hf, d - 1], s2s.at[a, hf, d - 1],
                    s2r.at[a, hf, d - 1], (ring(1 - hf, d), wa, col),
                )
                copy.start()
                twos[a, hf, d] = copy

    def third(a):
        for hf in range(2):
            for d in range(1, 4):
                twos[a, hf, d].wait_recv()
            total = q2[a, hf, mine[1 - hf]] + r2[a, hf, 0] + r2[a, hf, 1] + r2[a, hf, 2]
            for k in range(7):
                at = (7 * hf + k) * 8
                vs[a, at : at + 8, :] = total[:, k * 128 : (k + 1) * 128]
        y = []
        for i in range(6):
            tiles = jnp.concatenate([vs[a, pl.ds(j * 8 + i, 8, stride=24), :] for j in range(3)], axis=1)
            y.append((tiles[:, 0:CH], tiles[:, CH : 2 * CH]))
        for w in range(16):
            i0, o0 = (72 * w) // CH, (72 * w) % CH
            n0 = min(72, CH - o0)
            pieces = []
            for parity in range(2):
                pieces.append(y[i0][parity][:, o0 : o0 + n0])
                if n0 < 72:
                    pieces.append(y[i0 + 1][parity][:, 0 : 72 - n0])
            tile = jnp.concatenate(pieces, axis=1)
            zb[a, w] = tile[:, 0:128]
            spare = jnp.concatenate([tile[k : k + 1, 128:144] for k in range(4)], axis=1)
            zb[a, w, 5:6, 0:64] = spare

        def z_send(d, _):
            remote(
                zb.at[a, (wa + d) % 16], r3.at[a, d - 1], s3s.at[a, d - 1], s3r.at[a, d - 1],
                (ha, (wa + d) % 16, col),
            ).start()
            return 0

        lax.fori_loop(1, 16, z_send, 0)

    def finish(a):
        def z_wait(d, _):
            remote(
                zb.at[a, (wa + d) % 16], r3.at[a, d - 1], s3s.at[a, d - 1], s3r.at[a, d - 1],
                (ha, (wa + d) % 16, col),
            ).wait()
            return 0

        lax.fori_loop(1, 16, z_wait, 0)
        total = zb[a, wa] + jnp.sum(r3[a], axis=0)
        for be in range(9):
            k = be // 2
            if be % 2 == 0:
                row = total[k : k + 1, 0:72]
            else:
                row = jnp.concatenate([total[k : k + 1, 72:128], total[5:6, 16 * k : 16 * k + 16]], axis=1)
            gw_ref[9 * a + be] = row

    def gh_wait(d, _):
        src = (ha + 16 - d) % 16
        remote(gh.at[ha], gh.at[src], ghs.at[d - 1], ghr.at[d - 1], (src, wa, col)).wait_recv()
        return 0

    def gz_send(d, _):
        remote(gz.at[wa], gz.at[wa], gzs.at[d - 1], gzr.at[d - 1], (ha, (wa + d) % 16, col)).start()
        return 0

    def gz_wait(d, _):
        src = (wa + 16 - d) % 16
        remote(gz.at[wa], gz.at[src], gzs.at[d - 1], gzr.at[d - 1], (ha, src, col)).wait_recv()
        return 0

    second(0)
    second(1)
    lax.fori_loop(1, 16, gh_wait, 0)
    gz[wa] = jnp.sum(gh[...], axis=0)
    lax.fori_loop(1, 16, gz_send, 0)
    third(0)
    second(2)
    third(1)
    lax.fori_loop(1, 16, gz_wait, 0)
    gc[0] = jnp.sum(gz[...], axis=0)
    gc_copy = remote(gc.at[0], gc.at[1], gcs, gcr, (ha, wa, other))
    gc_copy.start()
    third(2)
    finish(0)
    gc_copy.wait()
    gg_ref[...] = (gc[0] + gc[1])[:, 0:CH]
    gg_out = pltpu.make_async_copy(gg_ref, gg_hbm, out_sem.at[1])
    gg_out.start()
    finish(1)
    finish(2)
    gw_out = pltpu.make_async_copy(gw_ref, gw_hbm, out_sem.at[2])
    gw_out.start()

    for copy in halos + d_copies + [u_copy] + list(ones.values()) + list(twos.values()):
        copy.wait_send()

    def g_done(d, _):
        remote(gh.at[ha], gh.at[ha], ghs.at[d - 1], ghr.at[d - 1], ((ha + d) % 16, wa, col)).wait_send()
        remote(gz.at[wa], gz.at[wa], gzs.at[d - 1], gzr.at[d - 1], (ha, (wa + d) % 16, col)).wait_send()
        return 0

    lax.fori_loop(1, 16, g_done, 0)
    for copy in (gi_out, gg_out, gw_out):
        copy.wait()


def hand_on(gi_from, gw_from, gg_from, gi_to, gw_to, gg_to, sem):
    copies = [
        pltpu.make_async_copy(src, dst, sem.at[n])
        for n, (src, dst) in enumerate(((gi_from, gi_to), (gw_from, gw_to), (gg_from, gg_to)))
    ]
    for copy in copies:
        copy.start()
    for copy in copies:
        copy.wait()


def on_device(inputs, carried, gain, weight, cotangent):
    hbm = pl.BlockSpec(memory_space=pl.ANY)
    dma = pltpu.SemaphoreType.DMA
    outs = (
        jax.ShapeDtypeStruct((T, S * CH), BF16),
        jax.ShapeDtypeStruct((27, 1, 72), F32),
        jax.ShapeDtypeStruct((1, CH), F32),
    )
    results = pl.pallas_call(
        kernel,
        out_shape=outs,
        in_specs=[hbm] * 5,
        out_specs=(pl.BlockSpec(memory_space=pltpu.VMEM),) * 3,
        scratch_shapes=[
            pltpu.VMEM((T, S * CH), BF16),
            pltpu.VMEM((27, 1, 72), F32),
            pltpu.VMEM((1, CH), F32),
            pltpu.VMEM((T, S * CH), BF16),
            pltpu.VMEM((2, S * CH), BF16),
            pltpu.VMEM((1, CH), F32),
            pltpu.VMEM((576, 128), BF16),
            pltpu.VMEM((576, 128), F32),
            pltpu.VMEM((2, 24, TP, 128), F32),
            pltpu.VMEM((2, 24, TP, 128), BF16),
            pltpu.VMEM((2, 24, TP, 128), BF16),
            pltpu.VMEM((2, 4, 2, TP, 128), BF16),
            pltpu.VMEM((27, CH * CH), BF16),
            pltpu.VMEM((4 * 288 * 8, 128), F32),
            pltpu.VMEM((768, 2 * HALF), BF16),
            pltpu.VMEM((S, 24, CH), F32),
            pltpu.VMEM((3, 2, 3, 96, ROWS), BF16),
            pltpu.VMEM((4 * ROWS, 2 * HALF), BF16),
            pltpu.VMEM((2, 3, 4, 24, HALF), F32),
            pltpu.VMEM((3, 2, 24, HALF), F32),
            pltpu.VMEM((3, 2, 2, 24, HALF), F32),
            pltpu.VMEM((3, 2, 24, HALF), F32),
            pltpu.VMEM((32, HALF), F32),
            pltpu.VMEM((3, 2, 4, 8, HALF), F32),
            pltpu.VMEM((3, 2, 3, 8, HALF), F32),
            pltpu.VMEM((3, 192, 128), F32),
            pltpu.VMEM((3, 16, 8, 128), F32),
            pltpu.VMEM((3, 15, 8, 128), F32),
            pltpu.VMEM((16, 1, 256), F32),
            pltpu.VMEM((16, 1, 256), F32),
            pltpu.VMEM((2, 1, 256), F32),
            dma((5,)), dma((3,)), dma((8,)), dma((8,)), dma((3,)), dma((3,)),
            dma((3, 2, 6)), dma((3, 2, 6)), dma((3, 2, 3)), dma((3, 2, 3)),
            dma((3, 15)), dma((3, 15)), dma((15,)), dma((15,)), dma((15,)), dma((15,)), dma(()), dma(()),
        ],
        compiler_params=pltpu.CompilerParams(
            collective_id=0, has_side_effects=True, vmem_limit_bytes=(65536 - 10400) * 1024
        ),
    )(
        inputs.reshape(T, S * CH),
        carried.reshape(2, S * CH),
        gain.reshape(1, CH),
        weight,
        cotangent.reshape(T, 2, 24, 128).transpose(0, 2, 1, 3).reshape(576, 128),
    )
    gi, gw, gg = pl.pallas_call(
        hand_on, out_shape=outs, in_specs=[pl.BlockSpec(memory_space=pl.ANY)] * 3, out_specs=(hbm, hbm, hbm), scratch_shapes=[dma((3,))],
        compiler_params=pltpu.CompilerParams(vmem_limit_bytes=16 * 1024 * 1024),
    )(*results)
    return gi.reshape(inputs.shape), gw.reshape(1, 27, 72), gg.reshape(CH)


def solution(mesh):
    placed = (
        P("col", None, "ha", "wa"),
        P("col", None, "ha", "wa"),
        P(),
        P(),
        P("col", None, "ha", "wa"),
    )
    return jax.shard_map(
        on_device,
        mesh=mesh,
        in_specs=placed,
        out_specs=(P("col", None, "ha", "wa"), P("col", None, ("ha", "wa")), P()),
        check_vma=False,
    )
```
